256 devices in a mesh: wide: 32 (over x, z), narrow: 8 (over y, core).
Axes of the slice: x: 4, y: 4, z: 8, core: 2. Of those that a mesh axis runs over, the one named last changes fastest.
Arguments:
- records: bfloat16 [32, 512, 49152], P(None, 'narrow', 'wide'), may hold values from -6 to 6
- taps: float32 [201], replicated, may hold values from -0.4375 to 0.4375
- pair_sources: int32 [32, 4], replicated, may hold values from 0 to 31, as said below
- pair_counts: int32 [32], P('wide'), may hold values from 1 to 4, as said below
Outputs:
- correlations: bfloat16 [32, 4, 512, 32, 256], P('wide', None, 'narrow')
The draws below stay inside these ranges and needn't reach their ends.
Inputs may be any that keep to these rules, and one draw needn't show every extreme that they name: `pair_sources`: each row lists 4 different blocks; only the first pair_counts[r] of row r are paired with r. `pair_counts`: some block has 4 pairs in every draw.
All inputs are finite; a program needn't handle non-finite values.
Results may differ from the reference program's by a relative error of at most 0.0096.
Values may be sent and summed in bfloat16 or wider, within the bound.
A program may use at most 128 MiB of HBM per device.

```python
import math
import jax
import jax.numpy as jnp
from jax import lax

BLOCK_CHANNELS = 512
VIRTUAL_SOURCES = 32
TAPS = 201
WLEN = 512
FREQUENCY_BINS = 128
F_LO = 4
LAG_COUNT = 256
MAX_PAIRED_SRC = 4
BLOCKS = 32
NWIN = 96
TIME = 49152


def draw_pair_sources(key, part):
    key = jax.random.fold_in(key, 11)
    scores = jax.random.randint(key, (BLOCKS, BLOCKS), 0, 1 << 30, dtype=jnp.int32)
    order = jnp.argsort(scores, axis=1, stable=True).astype(jnp.int32)
    return order[:, :MAX_PAIRED_SRC]


def draw_pair_counts(key, part):
    key = jax.random.fold_in(key, 23)
    first, second = jax.random.split(key)
    counts = jax.random.randint(first, (BLOCKS,), 1, MAX_PAIRED_SRC + 1, dtype=jnp.int32)
    fullest = jax.random.randint(second, (), 0, BLOCKS, dtype=jnp.int32)
    return counts.at[fullest].set(MAX_PAIRED_SRC)


def level_of(rng, shape, shards, smallest, largest):
    def one(position, blocks):
        steps = jax.random.uniform(jax.random.fold_in(jax.random.fold_in(rng, 6), position), (blocks,), jnp.float32, smallest / len(shards), largest / len(shards))
        return jnp.repeat(jnp.exp(steps), shape[position] // blocks).reshape((-1,) + (1,) * (len(shape) - position - 1))

    factor_of = one(*shards[0])
    for cut in shards[1:]:
        factor_of = factor_of * one(*cut)
    return factor_of


def normal_values(own_key, extent, spread, bound, shards=(), held_as=jnp.bfloat16):
    result = jax.random.normal(own_key, extent, jnp.float32) * spread
    if len(shards) > 0:
        result = level_of(own_key, extent, shards, -0.22, 0.18) * result
    return jnp.clip(result, min=-bound, max=bound).astype(held_as)


def setup_inputs(seed: int = 0) -> dict:
    keys = jax.random.split(jax.random.key(seed), 5)
    return {
        "records": normal_values(keys[0], (BLOCKS, BLOCK_CHANNELS, TIME), 1.0, 6.0, ((1, 8), (2, 32))),
        "taps": normal_values(keys[1], (TAPS,), TAPS ** -0.5, 0.4375, (), jnp.float32),
        "pair_sources": draw_pair_sources(jax.random.fold_in(keys[4], 71), 0),
        "pair_counts": draw_pair_counts(jax.random.fold_in(keys[4], 71), 0),
    }


def taps_matrix(taps):
    kernel = taps.astype(jnp.bfloat16)
    span = WLEN + TAPS - 1
    padded = jnp.concatenate([kernel[::-1], jnp.zeros((WLEN,), kernel.dtype)])
    tiled = jnp.tile(padded, WLEN)[:WLEN * span].reshape(WLEN, span)
    return tiled.T

def dft_table():
    times = jnp.arange(WLEN, dtype=jnp.int32)[:, None]
    bins = (F_LO + jnp.arange(FREQUENCY_BINS, dtype=jnp.int32))[None, :]
    phase = jnp.mod(times * bins, WLEN)
    angle = phase.astype(jnp.float32) * (2.0 * math.pi / WLEN)
    scale = 1.0 / math.sqrt(WLEN)
    return jnp.concatenate([jnp.cos(angle) * scale, -jnp.sin(angle) * scale], 1).astype(jnp.bfloat16)

def lag_table():
    bins = (F_LO + jnp.arange(FREQUENCY_BINS, dtype=jnp.int32))[:, None]
    lags = (jnp.arange(LAG_COUNT, dtype=jnp.int32) - LAG_COUNT // 2)[None, :]
    phase = jnp.mod(bins * lags, WLEN)
    angle = phase.astype(jnp.float32) * (2.0 * math.pi / WLEN)
    scale = 1.0 / math.sqrt(FREQUENCY_BINS)
    return jnp.concatenate([jnp.cos(angle) * scale, -jnp.sin(angle) * scale], 0).astype(jnp.bfloat16)

def cross_spectra(recv, source_indices, count):
    rec_re = recv[:, :, 0]
    rec_im = recv[:, :, 1]
    src_re = source_indices[:, :, :, 0]
    src_im = source_indices[:, :, :, 1]
    form = 'iwf,kjwf->kijf'
    real = jnp.einsum(form, rec_re, src_re, preferred_element_type=jnp.float32) + jnp.einsum(form, rec_im, src_im, preferred_element_type=jnp.float32)
    imag = jnp.einsum(form, rec_im, src_re, preferred_element_type=jnp.float32) - jnp.einsum(form, rec_re, src_im, preferred_element_type=jnp.float32)
    scale = 1.0 / math.sqrt(recv.shape[1])
    live = (jnp.arange(MAX_PAIRED_SRC, dtype=jnp.int32) < count).astype(jnp.float32)[:, None, None, None]
    return jnp.stack([real * scale * live, imag * scale * live], 3).astype(jnp.bfloat16)

def reference(records, taps, pair_sources, pair_counts):
    toeplitz = taps_matrix(taps)
    forward = dft_table()
    backward = lag_table()

    def block_spectra(block):
        main = block.reshape(BLOCK_CHANNELS, NWIN, WLEN)
        tails = main[:, :, WLEN - (TAPS - 1):]
        previous = jnp.concatenate([jnp.zeros((BLOCK_CHANNELS, 1, TAPS - 1), block.dtype), tails[:, :NWIN - 1]], 1)
        windows = jnp.concatenate([previous, main], 2)
        whitened = jnp.dot(windows, toeplitz, preferred_element_type=jnp.float32).astype(jnp.bfloat16)
        block_spectrum = jnp.dot(whitened, forward, preferred_element_type=jnp.float32).astype(jnp.bfloat16)
        return block_spectrum.reshape(BLOCK_CHANNELS, NWIN, 2, FREQUENCY_BINS)
    block_spectrum = lax.map(block_spectra, records)
    virtual_channels = block_spectrum[:, ::BLOCK_CHANNELS // VIRTUAL_SOURCES]

    def receiver(index):
        recv = block_spectrum[index].astype(jnp.float32)
        source_indices = jnp.take(virtual_channels, pair_sources[index], axis=0).astype(jnp.float32)
        cross = cross_spectra(recv, source_indices, pair_counts[index])
        lag_domain = jnp.dot(cross.reshape(-1, 2 * FREQUENCY_BINS), backward, preferred_element_type=jnp.float32)
        return lag_domain.astype(jnp.bfloat16).reshape(MAX_PAIRED_SRC, BLOCK_CHANNELS, VIRTUAL_SOURCES, LAG_COUNT)
    return lax.map(receiver, jnp.arange(BLOCKS, dtype=jnp.int32))
```

```python
import functools
import math

import jax
import jax.numpy as jnp
import ml_dtypes
import numpy as np
from jax import lax
from jax.experimental import pallas as pl
from jax.experimental.pallas import tpu as pltpu
from jax.sharding import PartitionSpec as P

TAPS = 201
WLEN = 512
BINS = 128
F_LO = 4
LAGS = 256
SLOTS = 4
HALF = 256
MESH = pl.DeviceIdType.MESH
BF = jnp.bfloat16
F32 = jnp.float32


def forward_table():
    times = np.arange(WLEN)[:, None]
    bins = (F_LO + np.arange(BINS))[None, :]
    angle = ((times * bins) % WLEN).astype(np.float32) * np.float32(2.0 * math.pi / WLEN)
    scale = np.float32(1.0 / math.sqrt(WLEN))
    table = np.concatenate([np.cos(angle) * scale, -np.sin(angle) * scale], 1)
    return table.astype(ml_dtypes.bfloat16)


def lag_table():
    bins = (F_LO + np.arange(BINS))[:, None]
    lags = (np.arange(LAGS) - LAGS // 2)[None, :]
    angle = ((bins * lags) % WLEN).astype(np.float32) * np.float32(2.0 * math.pi / WLEN)
    scale = np.float32(1.0 / math.sqrt(BINS))
    table = np.concatenate([np.cos(angle) * scale, -np.sin(angle) * scale], 0)
    return table.astype(ml_dtypes.bfloat16)


def dot(a, b, contract=((1,), (0,))):
    return lax.dot_general(a, b, (contract, ((), ())), preferred_element_type=F32)


NT = ((1,), (1,))
TN = ((0,), (0,))


def tables_kernel(windows, pairs_ref, counts_ref, taps_ref, toep_ref, pick_ref, scale_ref, pick):
    taps = taps_ref[...].astype(BF).astype(F32)
    width = taps.shape[1]
    rolled = pltpu.roll(jnp.broadcast_to(taps, (2 * HALF, width)), width - HALF, 1, stride=1, stride_axis=0)
    toep_ref[...] = rolled[:, :HALF].astype(BF)
    col = lax.broadcasted_iota(jnp.int32, (4, 128), 1)
    row = lax.broadcasted_iota(jnp.int32, (4, 128), 0)
    diff = col - row
    blocks = pairs_ref.shape[0]

    def fill(r, _):
        for k in range(SLOTS):
            first = pairs_ref[r, k] * 4
            pick[pl.ds(r * 16 + k * 4, 4), :] = jnp.where(diff == first, 1.0, 0.0).astype(F32)
        return 0

    lax.fori_loop(0, blocks, fill, 0)
    pick_ref[...] = pick[...].astype(BF)
    slot = lax.broadcasted_iota(jnp.int32, (8, 128), 1) // 32
    scale_ref[...] = jnp.where(slot < counts_ref[0], 1.0 / math.sqrt(windows), 0.0).astype(F32)


def spectra_kernel(
    rec_hbm, toep, fwd, fwd_t, extract, pick,
    r12, r0, s12, s0,
    rec, halo, z12, z0, vrec, p12, p0,
    load_sem, halo_sem, z_send, z_recv, p_send, p_recv, own_sem, b_send, b_recv, c_send, c_recv,
):
    wide, narrow = 32, 8
    me = lax.axis_index("wide")
    n = lax.axis_index("narrow")
    y, core = n // 2, lax.rem(n, 2)
    other = n + 1 - 2 * core
    groups = 8

    def load(g):
        return pltpu.make_async_copy(rec_hbm.at[pl.ds(g * 4, 4)], rec.at[pl.ds(g * 4, 4)], load_sem.at[g])

    for g in range(groups):
        load(g).start()

    barrier = pltpu.get_barrier_semaphore()

    def greet(o, _):
        pl.semaphore_signal(barrier, inc=1, device_id={"wide": lax.rem(me + o, wide)}, device_id_type=MESH)
        return 0

    lax.fori_loop(1, wide, greet, 0)
    y_peers = [lax.rem(y + d, 4) * 2 + core for d in range(4)]
    y_froms = [lax.rem(y + 4 - d, 4) * 2 for d in range(4)]
    for peer in y_peers[1:] + [other]:
        pl.semaphore_signal(barrier, inc=1, device_id={"narrow": peer}, device_id_type=MESH)
    pl.semaphore_wait(barrier, wide - 1 + 4)

    halo_copy = pltpu.make_async_remote_copy(
        src_ref=rec_hbm.at[:, :, pl.ds(1280, HALF)], dst_ref=halo, send_sem=halo_sem.at[0], recv_sem=halo_sem.at[1],
        device_id={"wide": lax.rem(me + 1, wide)}, device_id_type=MESH)
    halo_copy.start()

    def whiten(left, right):
        return (dot(left, toep[0:HALF, :]) + dot(right, toep[HALF:, :])).astype(BF)

    def send_sources(picked, landing, ws):
        def one(o, _):
            dst = lax.rem(me + o, wide)
            pltpu.make_async_remote_copy(
                src_ref=picked.at[dst], dst_ref=landing.at[n, me], send_sem=p_send.at[ws], recv_sem=p_recv.at[ws],
                device_id={"wide": dst}, device_id_type=MESH).start()
            return 0

        lax.fori_loop(1, wide, one, 0)
        pltpu.make_async_copy(picked.at[me], landing.at[n, me], own_sem.at[ws]).start()

    for g in range(groups):
        load(g).wait()
    for g in range(groups):
        block = rec[pl.ds(g * 4, 4)].reshape(256, 1536)
        vrec[pl.ds(g * 16, 16), :] = dot(extract[...], block).astype(BF)
    for w in (1, 2):
        parts = []
        for h in (2 * w, 2 * w + 1):
            parts.append(whiten(vrec[:, (h - 1) * HALF : h * HALF], vrec[:, h * HALF : (h + 1) * HALF]))
        v = (dot(parts[0], fwd[0:HALF, :]) + dot(parts[1], fwd[HALF:, :])).astype(BF)
        p12[:, :, (w - 1) * 256 : w * 256] = dot(pick[...], v).astype(BF).reshape(wide, 16, 256)
    send_sources(p12, s12, 0)

    left_half = lax.broadcasted_iota(jnp.int32, (128, 128), 1) < 64

    def transform(first, second, store):
        a = dot(fwd_t[:, 0:HALF], first, NT) + dot(fwd_t[:, HALF:], second, NT)
        for t in range(2):
            re, im = a[0:128, t * 128 : (t + 1) * 128], a[128:256, t * 128 : (t + 1) * 128]
            store(2 * t, jnp.where(left_half, re, pltpu.roll(im, 64, 1)).astype(BF))
            store(2 * t + 1, jnp.where(left_half, pltpu.roll(re, 64, 1), im).astype(BF))

    def send_spectra(z, landing, g, ws):
        for e in range(4):
            dst = g * 4 + e

            @pl.when(dst != me)
            def _():
                pltpu.make_async_remote_copy(
                    src_ref=z.at[dst], dst_ref=landing.at[me], send_sem=z_send.at[ws], recv_sem=z_recv.at[ws],
                    device_id={"wide": dst}, device_id_type=MESH).start()

            @pl.when(dst == me)
            def _():
                pltpu.make_async_copy(z.at[dst], landing.at[me], own_sem.at[2 + ws]).start()

    def group12(gi, _):
        g = lax.rem(me // 4 + gi, groups)
        x = rec[pl.ds(g * 4, 4)].reshape(256, 1536)
        for w in (1, 2):
            parts = []
            for h in (2 * w, 2 * w + 1):
                parts.append(whiten(x[:, (h - 1) * HALF : h * HALF], x[:, h * HALF : (h + 1) * HALF]))

            def store(e, value, w=w):
                z12[g * 4 + e, w - 1] = value

            transform(parts[0], parts[1], store)
        send_spectra(z12, r12, g, 0)
        return 0

    lax.fori_loop(0, groups, group12, 0)

    halo_copy.wait()
    later = jnp.where(me > 0, 1.0, 0.0).astype(BF)
    for g in range(groups):
        block = halo[pl.ds(g * 4, 4)].reshape(256, HALF)
        vrec[pl.ds(g * 16, 16), 2 * HALF : 3 * HALF] = dot(extract[...], block).astype(BF)
    first = whiten(vrec[:, 2 * HALF : 3 * HALF] * later, vrec[:, 0:HALF])
    second = whiten(vrec[:, 0:HALF], vrec[:, HALF : 2 * HALF])
    v = (dot(first, fwd[0:HALF, :]) + dot(second, fwd[HALF:, :])).astype(BF)
    p0[...] = dot(pick[...], v).astype(BF).reshape(wide, 16, 256)
    send_sources(p0, s0, 1)

    def group0(gi, _):
        g = lax.rem(me // 4 + gi, groups)
        h = halo[pl.ds(g * 4, 4)].reshape(256, HALF) * later
        x = rec[pl.ds(g * 4, 4), :, 0 : 2 * HALF].reshape(256, 2 * HALF)

        def store(e, value):
            z0[g * 4 + e] = value

        transform(whiten(h, x[:, 0:HALF]), whiten(x[:, 0:HALF], x[:, HALF:]), store)
        send_spectra(z0, r0, g, 1)
        return 0

    lax.fori_loop(0, groups, group0, 0)

    def arrived(landing, ws):
        pltpu.make_async_copy(landing.at[0, pl.ds(0, wide - 1)], landing.at[0, pl.ds(0, wide - 1)], p_recv.at[ws]).wait()
        pltpu.make_async_copy(landing.at[0, 0], landing.at[0, 0], own_sem.at[ws]).wait()

    def to_peer(landing, d, ws):
        return pltpu.make_async_remote_copy(
            src_ref=landing.at[n], dst_ref=landing.at[n], send_sem=b_send.at[ws, d], recv_sem=b_recv.at[ws, d],
            device_id={"narrow": y_peers[d] if d else other}, device_id_type=MESH)

    def across(landing, d, ws):
        piece = y_froms[d] + core
        return pltpu.make_async_remote_copy(
            src_ref=landing.at[piece], dst_ref=landing.at[piece], send_sem=c_send.at[ws, d], recv_sem=c_recv.at[ws, d],
            device_id={"narrow": other}, device_id_type=MESH)

    for ws, landing in ((0, s12), (1, s0)):
        arrived(landing, ws)
        for d in (1, 2, 3, 0):
            to_peer(landing, d, ws).start()
    for ws, landing in ((0, s12), (1, s0)):
        for d in (1, 3, 2):
            to_peer(landing, d, ws).wait_recv()
            across(landing, d, ws).start()
    for ws, landing in ((0, s12), (1, s0)):
        for d in range(4):
            to_peer(landing, d, ws).wait_send()
        to_peer(landing, 0, ws).wait_recv()
        for d in (1, 2, 3):
            across(landing, d, ws).wait()
    for ws, (z, p) in enumerate(((z12, p12), (z0, p0))):
        for sem, buf in ((p_send, p), (z_send, z), (z_recv, z)):
            part = buf.at[pl.ds(0, wide - 1)]
            pltpu.make_async_copy(part, part, sem.at[ws]).wait()
        pltpu.make_async_copy(z.at[0], z.at[0], own_sem.at[2 + ws]).wait()


def correlate_kernel(r12, r0, s12, s0, perm, lag, scale, out, rs, ss, cross):
    wide, rows = 32, 96
    rs[0 : 64 * 128, :] = r12[...].reshape(64 * 128, 128).astype(F32)
    rs[64 * 128 :, :] = r0[...].reshape(32 * 128, 128).astype(F32)

    def prepare(d, _):
        for w in range(3):
            if w < 2:
                s, j = s12[:, d, :, w * 256 : (w + 1) * 256], d * 2 + w
            else:
                s, j = s0[:, d], 64 + d
            st = dot(s.reshape(128, 256), perm[...], TN)
            start = pl.multiple_of(j * 128, 128)
            ss[0, pl.ds(start, 128), :] = st[0:128]
            ss[1, pl.ds(start, 128), :] = st[128:256]
        return 0

    lax.fori_loop(0, wide, prepare, 0, unroll=2)

    def one_bin(f, _):
        left = rs[pl.ds(f, rows, stride=128), :].T.astype(BF)
        turned = jnp.concatenate([left[64:128], -left[0:64]], 0)
        re = ss[0, pl.ds(f, rows, stride=128), :].astype(BF)
        im = ss[1, pl.ds(f, rows, stride=128), :].astype(BF)
        value = dot(left, re) + dot(turned, im)
        cross[pl.ds(pl.multiple_of(f * 128, 128), 128), :] = value * scale[0:1, :]
        return 0

    lax.fori_loop(0, BINS, one_bin, 0, unroll=4)

    def one_channel(i, _):
        x = jnp.concatenate(
            [cross[pl.ds(i, 128, stride=128), :], cross[pl.ds(64 + i, 128, stride=128), :]], 0).astype(BF)
        out[:, i] = dot(x, lag[...], TN).astype(BF).reshape(SLOTS, 32, LAGS)
        return 0

    lax.fori_loop(0, 64, one_channel, 0, unroll=2)


def on_device(records, taps, pair_sources, pair_counts):
    blocks, channels, _ = records.shape
    any_spec = pl.BlockSpec(memory_space=pl.ANY)
    vmem = pl.BlockSpec(memory_space=pltpu.VMEM)
    smem = pl.BlockSpec(memory_space=pltpu.SMEM)
    shape = jax.ShapeDtypeStruct
    taps_row = jnp.pad(taps, (0, 1024 - TAPS)).reshape(1, 1024)
    toep, pick, scale = pl.pallas_call(
        functools.partial(tables_kernel, 96),
        out_shape=(shape((512, 256), BF), shape((512, 128), BF), shape((8, 128), F32)),
        in_specs=[smem, smem, vmem],
        out_specs=(vmem, vmem, vmem),
        scratch_shapes=[pltpu.VMEM((512, 128), F32)],
        name="tables",
    )(pair_sources, pair_counts, taps_row)
    forward = forward_table()
    extract = np.zeros((16, 256), ml_dtypes.bfloat16)
    extract[np.arange(16), np.arange(16) * 16] = 1
    perm = np.zeros((128, 128), ml_dtypes.bfloat16)
    for col in range(128):
        k, v = col // 32, col % 32
        perm[(v // 4) * 16 + k * 4 + v % 4, col] = 1
    dma = pltpu.SemaphoreType.DMA
    r12, r0, s12, s0 = pl.pallas_call(
        spectra_kernel,
        out_shape=(
            shape((32, 2, 128, 128), BF), shape((32, 128, 128), BF),
            shape((8, 32, 16, 512), BF), shape((8, 32, 16, 256), BF)),
        in_specs=[any_spec, vmem, vmem, vmem, vmem, vmem],
        out_specs=(any_spec,) * 4,
        scratch_shapes=[
            pltpu.VMEM((blocks, channels, 1536), BF), pltpu.VMEM((blocks, channels, HALF), BF),
            pltpu.VMEM((32, 2, 128, 128), BF), pltpu.VMEM((32, 128, 128), BF),
            pltpu.VMEM((128, 1536), BF),
            pltpu.VMEM((32, 16, 512), BF), pltpu.VMEM((32, 16, 256), BF),
            dma((8,)), dma((2,)), dma((2,)), dma((2,)), dma((2,)), dma((2,)), dma((4,)),
            dma((2, 4)), dma((2, 4)), dma((2, 4)), dma((2, 4))],
        compiler_params=pltpu.CompilerParams(collective_id=0, has_side_effects=True, vmem_limit_bytes=40 << 20),
        name="spectra",
    )(records, toep, jnp.asarray(forward), jnp.asarray(forward.T), jnp.asarray(extract), pick)
    out = pl.pallas_call(
        correlate_kernel,
        out_shape=shape((SLOTS, channels, 32, LAGS), BF),
        in_specs=[vmem] * 7,
        out_specs=vmem,
        scratch_shapes=[
            pltpu.VMEM((96 * 128, 128), F32), pltpu.VMEM((2, 96 * 128, 128), F32), pltpu.VMEM((128 * 128, 128), F32)],
        compiler_params=pltpu.CompilerParams(vmem_limit_bytes=56 << 20),
        name="correlate",
    )(r12, r0, s12, s0, jnp.asarray(perm), jnp.asarray(lag_table()), scale)
    return out[None]


def solution(mesh):
    return jax.shard_map(
        on_device,
        mesh=mesh,
        in_specs=(P(None, "narrow", "wide"), P(), P(), P("wide")),
        out_specs=P("wide", None, "narrow", None, None),
        check_vma=False,
    )
```

```python
import math

import jax
import jax.numpy as jnp
import ml_dtypes
import numpy as np
from jax import lax
from jax.experimental import pallas as pl
from jax.experimental.pallas import tpu as pltpu
from jax.sharding import PartitionSpec as P

TAPS = 201
WLEN = 512
BINS = 128
F_LO = 4
LAGS = 256
SLOTS = 4
HALF = 256
PITCH = 136
CHUNKS = 4
STEP = BINS // CHUNKS
MESH = pl.DeviceIdType.MESH
BF = jnp.bfloat16
F32 = jnp.float32


def forward_table():
    times = np.arange(WLEN)[:, None]
    bins = (F_LO + np.arange(BINS))[None, :]
    angle = ((times * bins) % WLEN).astype(np.float32) * np.float32(2.0 * math.pi / WLEN)
    scale = np.float32(1.0 / math.sqrt(WLEN))
    table = np.concatenate([np.cos(angle) * scale, -np.sin(angle) * scale], 1)
    return table.astype(ml_dtypes.bfloat16)


def lag_table():
    bins = (F_LO + np.arange(BINS))[:, None]
    lags = (np.arange(LAGS) - LAGS // 2)[None, :]
    angle = ((bins * lags) % WLEN).astype(np.float32) * np.float32(2.0 * math.pi / WLEN)
    scale = np.float32(1.0 / math.sqrt(BINS))
    table = np.concatenate([np.cos(angle) * scale, -np.sin(angle) * scale], 0)
    return table.astype(ml_dtypes.bfloat16)


def dot(a, b, contract=((1,), (0,))):
    return lax.dot_general(a, b, (contract, ((), ())), preferred_element_type=F32)


NT = ((1,), (1,))
TN = ((0,), (0,))


def fill_tables(windows, taps, pairs, counts, repeat, taps_row, toep, pick, scale):
    taps_row[...] = jnp.zeros_like(taps_row)
    taps_row[:, 0:TAPS] = taps[...].astype(BF).astype(F32)
    width = taps_row.shape[1]
    rolled = pltpu.roll(
        jnp.broadcast_to(taps_row[...], (2 * HALF, width)), width - HALF, 1, stride=1, stride_axis=0)
    toep[...] = rolled[:, :HALF].astype(BF)
    every = dot(repeat[...], pairs[...].astype(F32).astype(BF), NT)
    lane = lax.broadcasted_iota(jnp.int32, (512, SLOTS), 1)
    slot = lax.rem(lax.broadcasted_iota(jnp.int32, (512, SLOTS), 0) // 4, SLOTS)
    source = jnp.sum(jnp.where(lane == slot, every, 0.0), axis=1, keepdims=True)
    col = lax.broadcasted_iota(jnp.int32, (512, 128), 1)
    row = lax.broadcasted_iota(jnp.int32, (512, 128), 0)
    same = lax.rem(col, 4) == lax.rem(row, 4)
    pick[...] = jnp.where(same & ((col // 4).astype(F32) == source), 1.0, 0.0).astype(BF)
    slot = lax.broadcasted_iota(jnp.int32, (8, 128), 1) // 32
    scale[...] = jnp.where(slot < counts[0], 1.0 / math.sqrt(windows), 0.0).astype(F32)


def whole_kernel(
    counts, rec_hbm, taps_hbm, pairs_hbm, fwd_hbm, fwd_t_hbm, extract_hbm, repeat_hbm, perm_hbm, lag_hbm,
    out_hbm,
    taps, pairs, fwd, fwd_t, extract, repeat, perm, lag, taps_row, toep, pick, scale,
    rec, halo, z12, z0, r12, r0, vrec, p12, p0, s12, s0, rs, ss, cross, out,
    const_sem, load_sem, halo_sem, z_send, z_recv, p_send, p_recv, own_sem, b_send, b_recv, c_send, c_recv, out_sem,
):
    wide, groups, rows = 32, 8, 96
    me = lax.axis_index("wide")
    n = lax.axis_index("narrow")
    y, core = n // 2, lax.rem(n, 2)
    other = n + 1 - 2 * core

    consts = [
        pltpu.make_async_copy(a, b, const_sem.at[i])
        for i, (a, b) in enumerate((
            (taps_hbm, taps), (pairs_hbm, pairs), (repeat_hbm, repeat), (extract_hbm, extract),
            (fwd_hbm, fwd), (fwd_t_hbm, fwd_t), (perm_hbm, perm), (lag_hbm, lag)))
    ]

    def load(g):
        return pltpu.make_async_copy(rec_hbm.at[pl.ds(g * 4, 4)], rec.at[pl.ds(g * 4, 4)], load_sem.at[g])

    for c in consts:
        c.start()
    for g in range(groups):
        load(g).start()

    barrier = pltpu.get_barrier_semaphore()

    def greet(o, _):
        pl.semaphore_signal(barrier, inc=1, device_id={"wide": lax.rem(me + o, wide)}, device_id_type=MESH)
        return 0

    lax.fori_loop(1, wide, greet, 0)
    y_peers = [lax.rem(y + d, 4) * 2 + core for d in range(4)]
    y_froms = [lax.rem(y + 4 - d, 4) * 2 for d in range(4)]
    for peer in y_peers[1:] + [other]:
        pl.semaphore_signal(barrier, inc=1, device_id={"narrow": peer}, device_id_type=MESH)

    for c in consts:
        c.wait()
    fill_tables(rows, taps, pairs, counts, repeat, taps_row, toep, pick, scale)
    pl.semaphore_wait(barrier, wide - 1 + 4)

    halo_copy = pltpu.make_async_remote_copy(
        src_ref=rec_hbm.at[:, :, pl.ds(1280, HALF)], dst_ref=halo, send_sem=halo_sem.at[0], recv_sem=halo_sem.at[1],
        device_id={"wide": lax.rem(me + 1, wide)}, device_id_type=MESH)
    halo_copy.start()

    def whiten(left, right):
        return (dot(left, toep[0:HALF, :]) + dot(right, toep[HALF:, :])).astype(BF)

    def send_sources(picked, landing, ws):
        def one(o, _):
            dst = lax.rem(me + o, wide)
            pltpu.make_async_remote_copy(
                src_ref=picked.at[dst], dst_ref=landing.at[n, me], send_sem=p_send.at[ws], recv_sem=p_recv.at[ws],
                device_id={"wide": dst}, device_id_type=MESH).start()
            return 0

        lax.fori_loop(1, wide, one, 0)
        pltpu.make_async_copy(picked.at[me], landing.at[n, me], own_sem.at[ws]).start()

    for g in range(groups):
        load(g).wait()
        block = rec[pl.ds(g * 4, 4)].reshape(256, 1536)
        vrec[pl.ds(g * 16, 16), :] = dot(extract[...], block).astype(BF)
    for w in (1, 2):
        parts = []
        for h in (2 * w, 2 * w + 1):
            parts.append(whiten(vrec[:, (h - 1) * HALF : h * HALF], vrec[:, h * HALF : (h + 1) * HALF]))
        v = (dot(parts[0], fwd[0:HALF, :]) + dot(parts[1], fwd[HALF:, :])).astype(BF)
        p12[:, :, (w - 1) * 256 : w * 256] = dot(pick[...], v).astype(BF).reshape(wide, 16, 256)
    send_sources(p12, s12, 0)

    left_half = lax.broadcasted_iota(jnp.int32, (128, 128), 1) < 64

    def transform(first, second, store):
        a = dot(fwd_t[:, 0:HALF], first, NT) + dot(fwd_t[:, HALF:], second, NT)
        for t in range(2):
            re, im = a[0:128, t * 128 : (t + 1) * 128], a[128:256, t * 128 : (t + 1) * 128]
            store(2 * t, jnp.where(left_half, re, pltpu.roll(im, 64, 1)).astype(BF))
            store(2 * t + 1, jnp.where(left_half, pltpu.roll(re, 64, 1), im).astype(BF))

    def piece(ref, lead, c):
        at = pl.ds(pl.multiple_of(c * STEP, STEP), STEP)
        return ref.at[lead, :, at] if len(ref.shape) == 4 else ref.at[lead, at]

    def send_piece(z, landing, dst, ws, c):
        pltpu.make_async_remote_copy(
            src_ref=piece(z, dst, c), dst_ref=piece(landing, me, c),
            send_sem=z_send.at[ws, c], recv_sem=z_recv.at[ws, c],
            device_id={"wide": dst}, device_id_type=MESH).start()

    def send_group(z, landing, g, ws, chunks):
        for e in range(4):
            dst = g * 4 + e

            @pl.when(dst != me)
            def _():
                for c in chunks:
                    send_piece(z, landing, dst, ws, c)

            @pl.when(dst == me)
            def _():
                pltpu.make_async_copy(z.at[dst], landing.at[me], own_sem.at[2 + ws]).start()

    def send_rest(z, landing, ws, c):
        def one(o, _):
            send_piece(z, landing, lax.rem(me + o, wide), ws, c)
            return 0

        lax.fori_loop(1, wide, one, 0)

    def group12(gi, _):
        g = lax.rem(me // 4 + gi, groups)
        x = rec[pl.ds(g * 4, 4)].reshape(256, 1536)
        for w in (1, 2):
            parts = []
            for h in (2 * w, 2 * w + 1):
                parts.append(whiten(x[:, (h - 1) * HALF : h * HALF], x[:, h * HALF : (h + 1) * HALF]))

            def store(e, value, w=w):
                z12[g * 4 + e, w - 1] = value

            transform(parts[0], parts[1], store)
        send_group(z12, r12, g, 0, (0, 1))
        return 0

    lax.fori_loop(0, groups, group12, 0)

    def arrived(landing, ws):
        some = landing.at[0, pl.ds(0, wide - 1)]
        pltpu.make_async_copy(some, some, p_recv.at[ws]).wait()
        pltpu.make_async_copy(landing.at[0, 0], landing.at[0, 0], own_sem.at[ws]).wait()

    def to_peer(landing, d, ws):
        return pltpu.make_async_remote_copy(
            src_ref=landing.at[n], dst_ref=landing.at[n], send_sem=b_send.at[ws, d], recv_sem=b_recv.at[ws, d],
            device_id={"narrow": y_peers[d] if d else other}, device_id_type=MESH)

    def across(landing, d, ws):
        part = y_froms[d] + core
        return pltpu.make_async_remote_copy(
            src_ref=landing.at[part], dst_ref=landing.at[part], send_sem=c_send.at[ws, d], recv_sem=c_recv.at[ws, d],
            device_id={"narrow": other}, device_id_type=MESH)

    def gather_start(landing, ws):
        arrived(landing, ws)
        for d in (1, 2, 3, 0):
            to_peer(landing, d, ws).start()

    def gather_across(landing, ws):
        for d in (1, 3, 2):
            to_peer(landing, d, ws).wait_recv()
            across(landing, d, ws).start()

    def gather_end(landing, ws):
        for d in range(4):
            to_peer(landing, d, ws).wait_send()
        to_peer(landing, 0, ws).wait_recv()
        for d in (1, 2, 3):
            across(landing, d, ws).wait()

    gather_start(s12, 0)

    halo_copy.wait()
    later = jnp.where(me > 0, 1.0, 0.0).astype(BF)
    for g in range(groups):
        block = halo[pl.ds(g * 4, 4)].reshape(256, HALF)
        vrec[pl.ds(g * 16, 16), 2 * HALF : 3 * HALF] = dot(extract[...], block).astype(BF)
    first = whiten(vrec[:, 2 * HALF : 3 * HALF] * later, vrec[:, 0:HALF])
    second = whiten(vrec[:, 0:HALF], vrec[:, HALF : 2 * HALF])
    v = (dot(first, fwd[0:HALF, :]) + dot(second, fwd[HALF:, :])).astype(BF)
    p0[...] = dot(pick[...], v).astype(BF).reshape(wide, 16, 256)
    send_sources(p0, s0, 1)

    def group0(gi, _):
        g = lax.rem(me // 4 + gi, groups)
        h = halo[pl.ds(g * 4, 4)].reshape(256, HALF) * later
        x = rec[pl.ds(g * 4, 4), :, 0 : 2 * HALF].reshape(256, 2 * HALF)

        def store(e, value):
            z0[g * 4 + e] = value

        transform(whiten(h, x[:, 0:HALF]), whiten(x[:, 0:HALF], x[:, HALF:]), store)
        send_group(z0, r0, g, 1, (0, 1))
        return 0

    lax.fori_loop(0, groups, group0, 0)
    for c in range(2, CHUNKS):
        send_rest(z12, r12, 0, c)
        send_rest(z0, r0, 1, c)

    def turn(s, j):
        st = dot(s.reshape(128, 256), perm[...], TN)
        start = pl.multiple_of(j * PITCH, 8)
        ss[0, pl.ds(start, 128), :] = st[0:128]
        ss[1, pl.ds(start, 128), :] = st[128:256]

    def turn12(d, _):
        for w in range(2):
            turn(s12[:, d, :, w * 256 : (w + 1) * 256], d * 2 + w)
        return 0

    def turn0(d, _):
        turn(s0[:, d], 64 + d)
        return 0

    gather_across(s12, 0)
    gather_start(s0, 1)
    gather_end(s12, 0)
    lax.fori_loop(0, wide, turn12, 0, unroll=2)
    gather_across(s0, 1)
    gather_end(s0, 1)
    lax.fori_loop(0, wide, turn0, 0, unroll=4)

    for ws, z in enumerate((z12, z0)):
        pltpu.make_async_copy(z.at[0], z.at[0], own_sem.at[2 + ws]).wait()

    def one_bin(f):
        left = rs[pl.ds(f, rows, stride=PITCH), :].T.astype(BF)
        turned = jnp.concatenate([left[64:128], -left[0:64]], 0)
        re = ss[0, pl.ds(f, rows, stride=PITCH), :].astype(BF)
        im = ss[1, pl.ds(f, rows, stride=PITCH), :].astype(BF)
        value = dot(left, re) + dot(turned, im)
        cross[pl.ds(pl.multiple_of(f * PITCH, 8), 128), :] = value * scale[0:1, :]

    def one_chunk(c, _):
        base = pl.multiple_of(c * STEP, STEP)
        for ws, landing in ((0, r12), (1, r0)):
            some = piece(landing, pl.ds(0, wide - 1), 0)
            pltpu.make_async_copy(some, some, z_recv.at[ws, c]).wait()

        def widen(d, _):
            for j, part in ((2 * d, r12.at[d, 0]), (2 * d + 1, r12.at[d, 1]), (64 + d, r0.at[d])):
                rs[pl.ds(pl.multiple_of(j * PITCH + base, 8), STEP), :] = part[pl.ds(base, STEP), :].astype(F32)
            return 0

        lax.fori_loop(0, wide, widen, 0, unroll=4)

        def some_bins(i, _):
            for u in range(16):
                one_bin(base + i * 16 + u)
            return 0

        lax.fori_loop(0, STEP // 16, some_bins, 0)
        return 0

    lax.fori_loop(0, CHUNKS, one_chunk, 0)

    def write(q):
        at = pl.ds(pl.multiple_of(q * 16, 16), 16)
        return pltpu.make_async_copy(out.at[:, at], out_hbm.at[:, at], out_sem.at[q])

    def channels(q, _):
        for u in range(16):
            i = q * 16 + u
            x = jnp.concatenate(
                [cross[pl.ds(i, 128, stride=PITCH), :], cross[pl.ds(64 + i, 128, stride=PITCH), :]], 0).astype(BF)
            out[:, i] = dot(x, lag[...], TN).astype(BF).reshape(SLOTS, 32, LAGS)
        write(q).start()
        return 0

    lax.fori_loop(0, 4, channels, 0)
    for ws, (z, p) in enumerate(((z12, p12), (z0, p0))):
        some = p.at[pl.ds(0, wide - 1)]
        pltpu.make_async_copy(some, some, p_send.at[ws]).wait()
        for c in range(CHUNKS):
            some = piece(z, pl.ds(0, wide - 1), c)
            pltpu.make_async_copy(some, some, z_send.at[ws, c]).wait()
    for q in range(4):
        write(q).wait()


def on_device(records, taps, pair_sources, pair_counts):
    blocks, channels, _ = records.shape
    any_spec = pl.BlockSpec(memory_space=pl.ANY)
    smem = pl.BlockSpec(memory_space=pltpu.SMEM)
    forward = forward_table()
    extract = np.zeros((16, 256), ml_dtypes.bfloat16)
    extract[np.arange(16), np.arange(16) * 16] = 1
    repeat = np.zeros((512, 32), ml_dtypes.bfloat16)
    repeat[np.arange(512), np.arange(512) // 16] = 1
    perm = np.zeros((128, 128), ml_dtypes.bfloat16)
    for col in range(128):
        k, v = col // 32, col % 32
        perm[(v // 4) * 16 + k * 4 + v % 4, col] = 1
    dma = pltpu.SemaphoreType.DMA
    vm = lambda *shape, dtype=BF: pltpu.VMEM(shape, dtype)
    out = pl.pallas_call(
        whole_kernel,
        out_shape=jax.ShapeDtypeStruct((SLOTS, channels, 32, LAGS), BF),
        in_specs=[smem] + [any_spec] * 9,
        out_specs=any_spec,
        scratch_shapes=[
            vm(1, TAPS, dtype=F32), vm(SLOTS, 32, dtype=jnp.int32), vm(512, 256), vm(256, 512), vm(16, 256),
            vm(512, 32), vm(128, 128), vm(256, 256), vm(1, 1024, dtype=F32), vm(512, 256), vm(512, 128),
            vm(8, 128, dtype=F32),
            vm(blocks, channels, 1536), vm(blocks, channels, HALF),
            vm(32, 2, 128, 128), vm(32, 128, 128), vm(32, 2, 128, 128), vm(32, 128, 128), vm(128, 1536),
            vm(32, 16, 512), vm(32, 16, 256), vm(8, 32, 16, 512), vm(8, 32, 16, 256),
            vm(96 * PITCH, 128, dtype=F32), vm(2, 96 * PITCH, 128, dtype=F32), vm(128 * PITCH, 128, dtype=F32),
            vm(SLOTS, channels, 32, LAGS),
            dma((8,)), dma((8,)), dma((2,)), dma((2, CHUNKS)), dma((2, CHUNKS)), dma((2,)), dma((2,)), dma((4,)),
            dma((2, 4)), dma((2, 4)), dma((2, 4)), dma((2, 4)), dma((4,))],
        compiler_params=pltpu.CompilerParams(collective_id=0, has_side_effects=True, vmem_limit_bytes=62 << 20),
        name="correlations",
    )(pair_counts, records, taps.reshape(1, TAPS), pair_sources.T, jnp.asarray(forward), jnp.asarray(forward.T),
      jnp.asarray(extract), jnp.asarray(repeat), jnp.asarray(perm), jnp.asarray(lag_table()))
    return out[None]


def solution(mesh):
    return jax.shard_map(
        on_device,
        mesh=mesh,
        in_specs=(P(None, "narrow", "wide"), P(), P(), P("wide")),
        out_specs=P("wide", None, "narrow", None, None),
        check_vma=False,
    )
```

```python
import math

import jax
import jax.numpy as jnp
import ml_dtypes
import numpy as np
from jax import lax
from jax.experimental import pallas as pl
from jax.experimental.pallas import tpu as pltpu
from jax.sharding import PartitionSpec as P

TAPS = 201
WLEN = 512
BINS = 128
F_LO = 4
LAGS = 256
SLOTS = 4
HALF = 256
PITCH = 136
PAST = 208
FIRST = 2
CHUNKS = ((0, 112), (112, 16))
MESH = pl.DeviceIdType.MESH
BF = jnp.bfloat16
F32 = jnp.float32


def forward_table():
    times = np.arange(WLEN)[:, None]
    bins = (F_LO + np.arange(BINS))[None, :]
    angle = ((times * bins) % WLEN).astype(np.float32) * np.float32(2.0 * math.pi / WLEN)
    scale = np.float32(1.0 / math.sqrt(WLEN))
    table = np.concatenate([np.cos(angle) * scale, -np.sin(angle) * scale], 1)
    return table.astype(ml_dtypes.bfloat16)


def lag_table():
    bins = (F_LO + np.arange(BINS))[:, None]
    lags = (np.arange(LAGS) - LAGS // 2)[None, :]
    angle = ((bins * lags) % WLEN).astype(np.float32) * np.float32(2.0 * math.pi / WLEN)
    scale = np.float32(1.0 / math.sqrt(BINS))
    table = np.concatenate([np.cos(angle) * scale, -np.sin(angle) * scale], 0)
    return table.astype(ml_dtypes.bfloat16)


def dot(a, b, contract=((1,), (0,))):
    return lax.dot_general(a, b, (contract, ((), ())), preferred_element_type=F32)


NT = ((1,), (1,))
TN = ((0,), (0,))


def fill_tables(windows, taps, pairs, counts, repeat, taps_row, toep, pick, scale):
    taps_row[...] = jnp.zeros_like(taps_row)
    taps_row[:, 0:TAPS] = taps[...].astype(BF).astype(F32)
    width = taps_row.shape[1]
    rolled = pltpu.roll(
        jnp.broadcast_to(taps_row[...], (2 * HALF, width)), width - HALF, 1, stride=1, stride_axis=0)
    toep[...] = rolled[:, :HALF].astype(BF)
    every = dot(repeat[...], pairs[...].astype(F32).astype(BF), NT)
    lane = lax.broadcasted_iota(jnp.int32, (512, SLOTS), 1)
    slot = lax.rem(lax.broadcasted_iota(jnp.int32, (512, SLOTS), 0) // 4, SLOTS)
    source = jnp.sum(jnp.where(lane == slot, every, 0.0), axis=1, keepdims=True)
    col = lax.broadcasted_iota(jnp.int32, (512, 128), 1)
    row = lax.broadcasted_iota(jnp.int32, (512, 128), 0)
    same = lax.rem(col, 4) == lax.rem(row, 4)
    pick[...] = jnp.where(same & ((col // 4).astype(F32) == source), 1.0, 0.0).astype(BF)
    slot = lax.broadcasted_iota(jnp.int32, (8, 128), 1) // 32
    scale[...] = jnp.where(slot < counts[0], 1.0 / math.sqrt(windows), 0.0).astype(F32)


def whole_kernel(
    counts, rec_hbm, taps_hbm, pairs_hbm, fwd_hbm, fwd_t_hbm, extract_hbm, repeat_hbm, perm_hbm, shift_hbm,
    out,
    taps, pairs, fwd, fwd_t, extract, repeat, perm, shift, taps_row, toep, pick, scale,
    rec, own_past, past, past_source, z12, z0, r12, r0, vrec, p12, p0, s12, s0, rs, ss, cross, turned_cross, relay,
    const_sem, load_sem, halo_sem, z_send, z_recv, p_send, p_recv, own_sem, b_send, b_recv, c_send, c_recv, relay_sem, onward_sem, out_sem,
):
    wide, groups, rows = 32, 8, 96
    me = lax.axis_index("wide")
    n = lax.axis_index("narrow")
    y, core = n // 2, lax.rem(n, 2)
    other = n + 1 - 2 * core

    consts = [
        pltpu.make_async_copy(a, b, const_sem.at[i])
        for i, (a, b) in enumerate((
            (taps_hbm, taps), (pairs_hbm, pairs), (repeat_hbm, repeat), (extract_hbm, extract),
            (shift_hbm, shift), (fwd_hbm, fwd), (fwd_t_hbm, fwd_t), (perm_hbm, perm)))
    ]

    def load(g):
        part = (pl.ds(g * 4, 4), slice(None), pl.ds(0, 1280))
        return pltpu.make_async_copy(rec_hbm.at[part], rec.at[part], load_sem.at[g])

    last = (slice(None), slice(None), pl.ds(1280, HALF))
    tails = pltpu.make_async_copy(rec_hbm.at[last], rec.at[last], load_sem.at[groups])
    tails.start()

    for c in consts:
        c.start()
    x, z_at = me // 8, lax.rem(me, 8)

    def group_at(gi):
        return lax.rem(x + gi, 4) * 2 + lax.rem(z_at // 4 + 1 + gi // 4, 2)

    for gi in range(groups):
        load(group_at(gi)).start()

    barrier = pltpu.get_barrier_semaphore()

    def greet(o, _):
        pl.semaphore_signal(barrier, inc=1, device_id={"wide": lax.rem(me + o, wide)}, device_id_type=MESH)
        return 0

    lax.fori_loop(1, wide, greet, 0)
    y_peers = [lax.rem(y + d, 4) * 2 + core for d in range(4)]
    y_froms = [lax.rem(y + 4 - d, 4) * 2 for d in range(4)]
    for peer in y_peers[1:] + [other]:
        pl.semaphore_signal(barrier, inc=1, device_id={"narrow": peer}, device_id_type=MESH)

    for c in consts:
        c.wait()
    fill_tables(rows, taps, pairs, counts, repeat, taps_row, toep, pick, scale)

    tails.wait()
    for g in range(groups):
        tail = rec[pl.ds(g * 4, 4), :, 1280:].reshape(256, HALF)
        own_past[:, g * 256 : (g + 1) * 256] = dot(shift[...], tail, NT).astype(BF)

    def whiten(left, right):
        return (dot(left, toep[0:HALF, :]) + dot(right, toep[HALF:, :])).astype(BF)

    def send_sources(picked, landing, ws):
        def one(o, _):
            dst = lax.rem(me + o, wide)
            pltpu.make_async_remote_copy(
                src_ref=picked.at[dst], dst_ref=landing.at[n, me], send_sem=p_send.at[ws], recv_sem=p_recv.at[ws],
                device_id={"wide": dst}, device_id_type=MESH).start()
            return 0

        lax.fori_loop(1, wide, one, 0)
        pltpu.make_async_copy(picked.at[me], landing.at[n, me], own_sem.at[ws]).start()

    left_half = lax.broadcasted_iota(jnp.int32, (128, 128), 1) < 64

    def transform(first, second, store):
        a = dot(fwd_t[:, 0:HALF], first, NT) + dot(fwd_t[:, HALF:], second, NT)
        for t in range(2):
            re, im = a[0:128, t * 128 : (t + 1) * 128], a[128:256, t * 128 : (t + 1) * 128]
            store(2 * t, jnp.where(left_half, re, pltpu.roll(im, 64, 1)).astype(BF))
            store(2 * t + 1, jnp.where(left_half, pltpu.roll(re, 64, 1), im).astype(BF))

    def piece(ref, lead, c):
        at = pl.ds(*CHUNKS[c])
        return ref.at[lead, :, at] if len(ref.shape) == 4 else ref.at[lead, at]

    def send_piece(z, landing, dst, ws, c):
        pltpu.make_async_remote_copy(
            src_ref=piece(z, dst, c), dst_ref=piece(landing, me, c),
            send_sem=z_send.at[ws, c], recv_sem=z_recv.at[ws, c],
            device_id={"wide": dst}, device_id_type=MESH).start()

    half_way, relay_to = lax.rem(z_at + 4, 8), x * 8 + lax.rem(z_at + 6, 8)

    def send_group(z, landing, g, ws):
        for e in range(4):
            dst = g * 4 + e
            far = (lax.rem(dst, 8) == half_way) if ws == 0 else False

            @pl.when((dst != me) & jnp.logical_not(far))
            def _():
                send_piece(z, landing, dst, ws, 0)

            if ws == 0:

                @pl.when(far)
                def _():
                    pltpu.make_async_remote_copy(
                        src_ref=piece(z, dst, 0), dst_ref=relay.at[lax.rem(dst // 8 + 4 - x, 4)],
                        send_sem=z_send.at[ws, 0], recv_sem=relay_sem,
                        device_id={"wide": relay_to}, device_id_type=MESH).start()

            @pl.when(dst == me)
            def _():
                pltpu.make_async_copy(z.at[dst], landing.at[me], own_sem.at[2 + ws]).start()

    def onward():
        pltpu.make_async_copy(relay, relay, relay_sem).wait()
        origin = x * 8 + lax.rem(z_at + 2, 8)
        for d in range(4):
            pltpu.make_async_remote_copy(
                src_ref=relay.at[d], dst_ref=piece(r12, origin, 0),
                send_sem=onward_sem, recv_sem=z_recv.at[0, 0],
                device_id={"wide": lax.rem(x + d, 4) * 8 + lax.rem(z_at + 6, 8)}, device_id_type=MESH).start()

    def send_rest(z, landing, ws, c):
        def one(o, _):
            send_piece(z, landing, lax.rem(me + o, wide), ws, c)
            return 0

        lax.fori_loop(1, wide, one, 0)

    def group12(gi, _):
        g = group_at(gi)
        x = rec[pl.ds(g * 4, 4)].reshape(256, 1536)
        for w in (1, 2):
            parts = []
            for h in (2 * w, 2 * w + 1):
                parts.append(whiten(x[:, (h - 1) * HALF : h * HALF], x[:, h * HALF : (h + 1) * HALF]))

            def store(e, value, w=w):
                z12[g * 4 + e, w - 1] = value

            transform(parts[0], parts[1], store)
        return 0

    def next12(gi, _):
        group12(gi, 0)
        return send12(gi, 0)

    def first12(gi, _):
        load(group_at(gi)).wait()
        return group12(gi, 0)

    lax.fori_loop(0, FIRST, first12, 0)

    pl.semaphore_wait(barrier, wide - 1 + 4)
    past_copy = pltpu.make_async_remote_copy(
        src_ref=own_past, dst_ref=past, send_sem=halo_sem.at[0], recv_sem=halo_sem.at[1],
        device_id={"wide": lax.rem(me + 1, wide)}, device_id_type=MESH)
    past_copy.start()

    def send12(gi, _):
        send_group(z12, r12, group_at(gi), 0)
        return 0

    lax.fori_loop(0, FIRST, send12, 0)

    for gi in range(FIRST, groups):
        load(group_at(gi)).wait()
    for g in range(groups):
        block = rec[pl.ds(g * 4, 4)].reshape(256, 1536)
        vrec[pl.ds(g * 16, 16), :] = dot(extract[...], block).astype(BF)
    for w in (1, 2):
        parts = []
        for h in (2 * w, 2 * w + 1):
            parts.append(whiten(vrec[:, (h - 1) * HALF : h * HALF], vrec[:, h * HALF : (h + 1) * HALF]))
        v = (dot(parts[0], fwd[0:HALF, :]) + dot(parts[1], fwd[HALF:, :])).astype(BF)
        p12[:, :, (w - 1) * 256 : w * 256] = dot(pick[...], v).astype(BF).reshape(wide, 16, 256)
    send_sources(p12, s12, 0)

    lax.fori_loop(FIRST, groups, next12, 0)

    def arrived(landing, ws):
        some = landing.at[0, pl.ds(0, wide - 1)]
        pltpu.make_async_copy(some, some, p_recv.at[ws]).wait()
        pltpu.make_async_copy(landing.at[0, 0], landing.at[0, 0], own_sem.at[ws]).wait()

    def to_peer(landing, d, ws):
        return pltpu.make_async_remote_copy(
            src_ref=landing.at[n], dst_ref=landing.at[n], send_sem=b_send.at[ws, d], recv_sem=b_recv.at[ws, d],
            device_id={"narrow": y_peers[d] if d else other}, device_id_type=MESH)

    def across(landing, d, ws):
        part = y_froms[d] + core
        return pltpu.make_async_remote_copy(
            src_ref=landing.at[part], dst_ref=landing.at[part], send_sem=c_send.at[ws, d], recv_sem=c_recv.at[ws, d],
            device_id={"narrow": other}, device_id_type=MESH)

    def gather_start(landing, ws):
        arrived(landing, ws)
        for d in (1, 2, 3, 0):
            to_peer(landing, d, ws).start()

    def gather_across(landing, ws):
        for d in (1, 3, 2):
            to_peer(landing, d, ws).wait_recv()
            across(landing, d, ws).start()

    def gather_end(landing, ws):
        for d in range(4):
            to_peer(landing, d, ws).wait_send()
        to_peer(landing, 0, ws).wait_recv()
        for d in (1, 2, 3):
            across(landing, d, ws).wait()

    onward()

    past_copy.wait()
    later = jnp.where(me > 0, 1.0, 0.0).astype(F32)

    def whiten_past(left, right, contract):
        return (dot(left, toep[HALF - PAST : HALF, :], contract) * later + dot(right, toep[HALF:, :])).astype(BF)

    for g in range(groups):
        block = past[:, g * 256 : (g + 1) * 256]
        past_source[pl.ds(g * 16, 16), 0:PAST] = dot(extract[...], block, NT).astype(BF)
    first = whiten_past(past_source[:, 0:PAST], vrec[:, 0:HALF], ((1,), (0,)))
    second = whiten(vrec[:, 0:HALF], vrec[:, HALF : 2 * HALF])
    v = (dot(first, fwd[0:HALF, :]) + dot(second, fwd[HALF:, :])).astype(BF)
    p0[...] = dot(pick[...], v).astype(BF).reshape(wide, 16, 256)
    send_sources(p0, s0, 1)

    def group0(gi, _):
        g = group_at(gi)
        h = past[:, pl.ds(pl.multiple_of(g * 256, 256), 256)]
        x = rec[pl.ds(g * 4, 4), :, 0 : 2 * HALF].reshape(256, 2 * HALF)

        def store(e, value):
            z0[g * 4 + e] = value

        transform(whiten_past(h, x[:, 0:HALF], TN), whiten(x[:, 0:HALF], x[:, HALF:]), store)
        send_group(z0, r0, g, 1)
        return 0

    lax.fori_loop(0, groups, group0, 0)
    send_rest(z12, r12, 0, 1)
    send_rest(z0, r0, 1, 1)
    gather_start(s12, 0)

    def turn(s, j):
        st = dot(s.reshape(128, 256), perm[...], TN)
        start = pl.multiple_of(j * PITCH, 8)
        ss[0, pl.ds(start, 128), :] = st[0:128]
        ss[1, pl.ds(start, 128), :] = st[128:256]

    def turn12(d, _):
        for w in range(2):
            turn(s12[:, d, :, w * 256 : (w + 1) * 256], d * 2 + w)
        return 0

    def turn0(d, _):
        turn(s0[:, d], 64 + d)
        return 0

    gather_across(s12, 0)
    gather_start(s0, 1)
    gather_end(s12, 0)
    lax.fori_loop(0, wide, turn12, 0, unroll=2)
    gather_across(s0, 1)
    gather_end(s0, 1)
    lax.fori_loop(0, wide, turn0, 0, unroll=4)

    for ws, z in enumerate((z12, z0)):
        pltpu.make_async_copy(z.at[0], z.at[0], own_sem.at[2 + ws]).wait()

    def one_bin(f):
        left = rs[pl.ds(f, rows, stride=PITCH), :].T.astype(BF)
        turned = jnp.concatenate([left[64:128], -left[0:64]], 0)
        re = ss[0, pl.ds(f, rows, stride=PITCH), :].astype(BF)
        im = ss[1, pl.ds(f, rows, stride=PITCH), :].astype(BF)
        value = dot(left, re) + dot(turned, im)
        cross[pl.ds(pl.multiple_of(f * PITCH, 8), 128), :] = value * scale[0:1, :]

    def write(c):
        at = pl.ds(*CHUNKS[c])
        return pltpu.make_async_copy(turned_cross.at[:, :, at], out.at[:, :, at], out_sem.at[c])

    for c, (base, step) in enumerate(CHUNKS):
        for ws, landing in ((0, r12), (1, r0)):
            some = piece(landing, pl.ds(0, wide - 1), c)
            pltpu.make_async_copy(some, some, z_recv.at[ws, c]).wait()

        def widen(d, _, base=base, step=step):
            for j, part in ((2 * d, r12.at[d, 0]), (2 * d + 1, r12.at[d, 1]), (64 + d, r0.at[d])):
                rs[pl.ds(pl.multiple_of(j * PITCH + base, 8), step), :] = part[base : base + step, :].astype(F32)
            return 0

        lax.fori_loop(0, wide, widen, 0, unroll=4)

        def some_bins(i, _, base=base):
            for u in range(16):
                one_bin(base + i * 16 + u)
            return 0

        lax.fori_loop(0, step // 16, some_bins, 0)
        def regroup(i, _, base=base, step=step):
            for p in range(2):
                rows_of = cross[pl.ds(base * PITCH + p * 64 + i, step, stride=PITCH), :]
                turned_cross[i, p, base : base + step, :] = rows_of.astype(BF)
            return 0

        lax.fori_loop(0, 64, regroup, 0, unroll=8)
        write(c).start()

    pltpu.make_async_copy(relay, relay, onward_sem).wait()
    for ws, (z, p) in enumerate(((z12, p12), (z0, p0))):
        some = p.at[pl.ds(0, wide - 1)]
        pltpu.make_async_copy(some, some, p_send.at[ws]).wait()
        for c in range(len(CHUNKS)):
            some = piece(z, pl.ds(0, wide - 1), c)
            pltpu.make_async_copy(some, some, z_send.at[ws, c]).wait()
    for c in range(len(CHUNKS)):
        write(c).wait()


def lag_kernel(cross_hbm, lag_hbm, out_hbm, cross, lag, out, lag_sem, read_sem, write_sem):
    channels, parts = cross.shape[0], 4
    each = channels // parts

    def read(q):
        at = pl.ds(q * each, each)
        return pltpu.make_async_copy(cross_hbm.at[at], cross.at[at], read_sem.at[q])

    def write(q):
        at = pl.ds(q * each, each)
        return pltpu.make_async_copy(out.at[:, at], out_hbm.at[:, at], write_sem.at[q])

    table = pltpu.make_async_copy(lag_hbm, lag, lag_sem)
    table.start()
    for q in range(parts):
        read(q).start()
    table.wait()
    for q in range(parts):
        read(q).wait()
        for i in range(q * each, (q + 1) * each):
            x = cross[i].reshape(2 * BINS, 128)
            out[:, i] = dot(x, lag[...], TN).astype(BF).reshape(SLOTS, 32, LAGS)
        write(q).start()
    for q in range(parts):
        write(q).wait()


def on_device(records, taps, pair_sources, pair_counts):
    blocks, channels, _ = records.shape
    any_spec = pl.BlockSpec(memory_space=pl.ANY)
    smem = pl.BlockSpec(memory_space=pltpu.SMEM)
    forward = forward_table()
    extract = np.zeros((16, 256), ml_dtypes.bfloat16)
    extract[np.arange(16), np.arange(16) * 16] = 1
    repeat = np.zeros((512, 32), ml_dtypes.bfloat16)
    repeat[np.arange(512), np.arange(512) // 16] = 1
    perm = np.zeros((128, 128), ml_dtypes.bfloat16)
    for col in range(128):
        k, v = col // 32, col % 32
        perm[(v // 4) * 16 + k * 4 + v % 4, col] = 1
    shift = np.zeros((PAST, HALF), ml_dtypes.bfloat16)
    shift[np.arange(PAST), HALF - PAST + np.arange(PAST)] = 1
    dma = pltpu.SemaphoreType.DMA
    vm = lambda *shape, dtype=BF: pltpu.VMEM(shape, dtype)
    cross = pl.pallas_call(
        whole_kernel,
        out_shape=jax.ShapeDtypeStruct((channels, 2, BINS, 128), BF),
        in_specs=[smem] + [any_spec] * 9,
        out_specs=any_spec,
        scratch_shapes=[
            vm(1, TAPS, dtype=F32), vm(SLOTS, 32, dtype=jnp.int32), vm(512, 256), vm(256, 512), vm(16, 256),
            vm(512, 32), vm(128, 128), vm(PAST, HALF), vm(1, 1024, dtype=F32), vm(512, 256), vm(512, 128),
            vm(8, 128, dtype=F32),
            vm(blocks, channels, 1536), vm(PAST, blocks * channels), vm(PAST, blocks * channels), vm(128, HALF),
            vm(32, 2, 128, 128), vm(32, 128, 128), vm(32, 2, 128, 128), vm(32, 128, 128), vm(128, 1536),
            vm(32, 16, 512), vm(32, 16, 256), vm(8, 32, 16, 512), vm(8, 32, 16, 256),
            vm(96 * PITCH, 128, dtype=F32), vm(2, 96 * PITCH, 128, dtype=F32), vm(BINS * PITCH, 128, dtype=F32),
            vm(channels, 2, BINS, 128), vm(4, 2, CHUNKS[0][1], 128),
            dma((8,)), dma((9,)), dma((2,)), dma((2, len(CHUNKS))), dma((2, len(CHUNKS))), dma((2,)), dma((2,)), dma((4,)),
            dma((2, 4)), dma((2, 4)), dma((2, 4)), dma((2, 4)), dma, dma, dma((len(CHUNKS),))],
        compiler_params=pltpu.CompilerParams(collective_id=0, has_side_effects=True, vmem_limit_bytes=62 << 20),
        name="cross",
    )(pair_counts, records, taps.reshape(1, TAPS), pair_sources.T, jnp.asarray(forward), jnp.asarray(forward.T),
      jnp.asarray(extract), jnp.asarray(repeat), jnp.asarray(perm), jnp.asarray(shift))
    out = pl.pallas_call(
        lag_kernel,
        out_shape=jax.ShapeDtypeStruct((SLOTS, channels, 32, LAGS), BF),
        in_specs=[any_spec, any_spec],
        out_specs=any_spec,
        scratch_shapes=[
            vm(channels, 2, BINS, 128), vm(2 * BINS, LAGS), vm(SLOTS, channels, 32, LAGS), dma, dma((4,)), dma((4,))],
        compiler_params=pltpu.CompilerParams(vmem_limit_bytes=60 << 20),
        name="lags",
    )(cross, jnp.asarray(lag_table()))
    return out[None]


def solution(mesh):
    return jax.shard_map(
        on_device,
        mesh=mesh,
        in_specs=(P(None, "narrow", "wide"), P(), P(), P("wide")),
        out_specs=P("wide", None, "narrow", None, None),
        check_vma=False,
    )
```

```python
import math

import jax
import jax.numpy as jnp
import ml_dtypes
import numpy as np
from jax import lax
from jax.experimental import pallas as pl
from jax.experimental.pallas import tpu as pltpu
from jax.sharding import PartitionSpec as P

TAPS = 201
WLEN = 512
BINS = 128
F_LO = 4
LAGS = 256
SLOTS = 4
HALF = 256
PITCH = 136
PAST = 208
FIRST = 1
CHUNKS = ((0, 96), (96, 32))
MESH = pl.DeviceIdType.MESH
BF = jnp.bfloat16
F32 = jnp.float32


def forward_table():
    times = np.arange(WLEN)[:, None]
    bins = (F_LO + np.arange(BINS))[None, :]
    angle = ((times * bins) % WLEN).astype(np.float32) * np.float32(2.0 * math.pi / WLEN)
    scale = np.float32(1.0 / math.sqrt(WLEN))
    table = np.concatenate([np.cos(angle) * scale, -np.sin(angle) * scale], 1)
    return table.astype(ml_dtypes.bfloat16)


def lag_table():
    bins = (F_LO + np.arange(BINS))[:, None]
    lags = (np.arange(LAGS) - LAGS // 2)[None, :]
    angle = ((bins * lags) % WLEN).astype(np.float32) * np.float32(2.0 * math.pi / WLEN)
    scale = np.float32(1.0 / math.sqrt(BINS))
    table = np.concatenate([np.cos(angle) * scale, -np.sin(angle) * scale], 0)
    return table.astype(ml_dtypes.bfloat16)


def dot(a, b, contract=((1,), (0,))):
    return lax.dot_general(a, b, (contract, ((), ())), preferred_element_type=F32)


NT = ((1,), (1,))
TN = ((0,), (0,))


def fill_filter(taps, taps_row, toep):
    taps_row[...] = jnp.zeros_like(taps_row)
    taps_row[:, 0:TAPS] = taps[...].astype(BF).astype(F32)
    width = taps_row.shape[1]
    rolled = pltpu.roll(
        jnp.broadcast_to(taps_row[...], (2 * HALF, width)), width - HALF, 1, stride=1, stride_axis=0)
    toep[...] = rolled[:, :HALF].astype(BF)


def fill_picks(windows, pairs, counts, repeat, pick, scale):
    every = dot(repeat[...], pairs[...].astype(F32).astype(BF), NT)
    lane = lax.broadcasted_iota(jnp.int32, (512, SLOTS), 1)
    slot = lax.rem(lax.broadcasted_iota(jnp.int32, (512, SLOTS), 0) // 4, SLOTS)
    source = jnp.sum(jnp.where(lane == slot, every, 0.0), axis=1, keepdims=True)
    col = lax.broadcasted_iota(jnp.int32, (512, 128), 1)
    row = lax.broadcasted_iota(jnp.int32, (512, 128), 0)
    same = lax.rem(col, 4) == lax.rem(row, 4)
    pick[...] = jnp.where(same & ((col // 4).astype(F32) == source), 1.0, 0.0).astype(BF)
    slot = lax.broadcasted_iota(jnp.int32, (8, 128), 1) // 32
    scale[...] = jnp.where(slot < counts[0], 1.0 / math.sqrt(windows), 0.0).astype(F32)


def whole_kernel(
    counts, rec_hbm, taps_hbm, pairs_hbm, fwd_hbm, fwd_t_hbm, extract_hbm, repeat_hbm, perm_hbm, shift_hbm,
    out,
    taps, pairs, fwd, fwd_t, extract, repeat, perm, shift, taps_row, toep, pick, scale,
    rec, own_past, past, past_source, z12, z0, r12, r0, vrec, p12, p0, s12, s0, rs, ss, cross, turned_cross, relay,
    const_sem, load_sem, halo_sem, z_send, z_recv, p_send, p_recv, own_sem, b_send, b_recv, c_send, c_recv, relay_sem, onward_sem, out_sem,
):
    wide, groups, rows = 32, 8, 96
    me = lax.axis_index("wide")
    n = lax.axis_index("narrow")
    y, core = n // 2, lax.rem(n, 2)
    other = n + 1 - 2 * core

    consts = [
        pltpu.make_async_copy(a, b, const_sem.at[i])
        for i, (a, b) in enumerate((
            (taps_hbm, taps), (fwd_t_hbm, fwd_t), (shift_hbm, shift), (extract_hbm, extract), (pairs_hbm, pairs),
            (repeat_hbm, repeat), (fwd_hbm, fwd), (perm_hbm, perm)))
    ]

    def load(g):
        part = (pl.ds(g * 4, 4), slice(None), pl.ds(0, 1280))
        return pltpu.make_async_copy(rec_hbm.at[part], rec.at[part], load_sem.at[g])

    last = (slice(None), slice(None), pl.ds(1280, HALF))
    tails = pltpu.make_async_copy(rec_hbm.at[last], rec.at[last], load_sem.at[groups])

    for c in consts[0:2]:
        c.start()
    tails.start()
    x, z_at = me // 8, lax.rem(me, 8)

    def group_at(gi):
        return lax.rem(x + gi, 4) * 2 + lax.rem(z_at // 4 + 1 + gi // 4, 2)

    for gi in range(groups):
        load(group_at(gi)).start()
        if gi == 0:
            for c in consts[2:]:
                c.start()

    barrier = pltpu.get_barrier_semaphore()

    def greet(o, _):
        pl.semaphore_signal(barrier, inc=1, device_id={"wide": lax.rem(me + o, wide)}, device_id_type=MESH)
        return 0

    lax.fori_loop(1, wide, greet, 0)
    y_peers = [lax.rem(y + d, 4) * 2 + core for d in range(4)]
    y_froms = [lax.rem(y + 4 - d, 4) * 2 for d in range(4)]
    for peer in y_peers[1:] + [other]:
        pl.semaphore_signal(barrier, inc=1, device_id={"narrow": peer}, device_id_type=MESH)

    for c in consts[0:2]:
        c.wait()
    fill_filter(taps, taps_row, toep)

    def whiten(left, right):
        return (dot(left, toep[0:HALF, :]) + dot(right, toep[HALF:, :])).astype(BF)

    def send_sources(picked, landing, ws):
        def one(o, _):
            dst = lax.rem(me + o, wide)
            pltpu.make_async_remote_copy(
                src_ref=picked.at[dst], dst_ref=landing.at[n, me], send_sem=p_send.at[ws], recv_sem=p_recv.at[ws],
                device_id={"wide": dst}, device_id_type=MESH).start()
            return 0

        lax.fori_loop(1, wide, one, 0)
        pltpu.make_async_copy(picked.at[me], landing.at[n, me], own_sem.at[ws]).start()

    left_half = lax.broadcasted_iota(jnp.int32, (128, 128), 1) < 64

    def transform(first, second, store):
        a = dot(fwd_t[:, 0:HALF], first, NT) + dot(fwd_t[:, HALF:], second, NT)
        for t in range(2):
            re, im = a[0:128, t * 128 : (t + 1) * 128], a[128:256, t * 128 : (t + 1) * 128]
            store(2 * t, jnp.where(left_half, re, pltpu.roll(im, 64, 1)).astype(BF))
            store(2 * t + 1, jnp.where(left_half, pltpu.roll(re, 64, 1), im).astype(BF))

    def piece(ref, lead, c):
        at = pl.ds(*CHUNKS[c])
        return ref.at[lead, :, at] if len(ref.shape) == 4 else ref.at[lead, at]

    def send_piece(z, landing, dst, ws, c):
        pltpu.make_async_remote_copy(
            src_ref=piece(z, dst, c), dst_ref=piece(landing, me, c),
            send_sem=z_send.at[ws, c], recv_sem=z_recv.at[ws, c],
            device_id={"wide": dst}, device_id_type=MESH).start()

    half_way, relay_to = lax.rem(z_at + 4, 8), x * 8 + lax.rem(z_at + 6, 8)

    def send_group(z, landing, g, ws):
        for e in range(4):
            dst = g * 4 + e
            far = (lax.rem(dst, 8) == half_way) if ws == 0 else False

            @pl.when((dst != me) & jnp.logical_not(far))
            def _():
                send_piece(z, landing, dst, ws, 0)

            if ws == 0:

                @pl.when(far)
                def _():
                    pltpu.make_async_remote_copy(
                        src_ref=piece(z, dst, 0), dst_ref=relay.at[lax.rem(dst // 8 + 4 - x, 4)],
                        send_sem=z_send.at[ws, 0], recv_sem=relay_sem,
                        device_id={"wide": relay_to}, device_id_type=MESH).start()

            @pl.when(dst == me)
            def _():
                pltpu.make_async_copy(z.at[dst], landing.at[me], own_sem.at[2 + ws]).start()

    def onward():
        pltpu.make_async_copy(relay, relay, relay_sem).wait()
        origin = x * 8 + lax.rem(z_at + 2, 8)
        for d in range(4):
            pltpu.make_async_remote_copy(
                src_ref=relay.at[d], dst_ref=piece(r12, origin, 0),
                send_sem=onward_sem, recv_sem=z_recv.at[0, 0],
                device_id={"wide": lax.rem(x + d, 4) * 8 + lax.rem(z_at + 6, 8)}, device_id_type=MESH).start()

    def send_rest(z, landing, ws, c):
        def one(o, _):
            send_piece(z, landing, lax.rem(me + o, wide), ws, c)
            return 0

        lax.fori_loop(1, wide, one, 0)

    def group12(gi, _):
        g = group_at(gi)
        x = rec[pl.ds(g * 4, 4)].reshape(256, 1536)
        for w in (1, 2):
            parts = []
            for h in (2 * w, 2 * w + 1):
                parts.append(whiten(x[:, (h - 1) * HALF : h * HALF], x[:, h * HALF : (h + 1) * HALF]))

            def store(e, value, w=w):
                z12[g * 4 + e, w - 1] = value

            transform(parts[0], parts[1], store)
        return 0

    def send12(gi, _):
        send_group(z12, r12, group_at(gi), 0)
        return 0

    def next12(gi, _):
        group12(gi, 0)
        return send12(gi, 0)

    def first12(gi, _):
        load(group_at(gi)).wait()
        return group12(gi, 0)

    tails.wait()
    lax.fori_loop(0, FIRST, first12, 0)

    pl.semaphore_wait(barrier, wide - 1 + 4)
    lax.fori_loop(0, FIRST, send12, 0)

    for c in consts[2:]:
        c.wait()
    for g in range(groups):
        tail = rec[pl.ds(g * 4, 4), :, 1280:].reshape(256, HALF)
        own_past[:, g * 256 : (g + 1) * 256] = dot(shift[...], tail, NT).astype(BF)
    past_copy = pltpu.make_async_remote_copy(
        src_ref=own_past, dst_ref=past, send_sem=halo_sem.at[0], recv_sem=halo_sem.at[1],
        device_id={"wide": lax.rem(me + 1, wide)}, device_id_type=MESH)
    past_copy.start()
    fill_picks(rows, pairs, counts, repeat, pick, scale)

    for gi in range(FIRST, groups):
        load(group_at(gi)).wait()
    for g in range(groups):
        block = rec[pl.ds(g * 4, 4)].reshape(256, 1536)
        vrec[pl.ds(g * 16, 16), :] = dot(extract[...], block).astype(BF)
    for w in (1, 2):
        parts = []
        for h in (2 * w, 2 * w + 1):
            parts.append(whiten(vrec[:, (h - 1) * HALF : h * HALF], vrec[:, h * HALF : (h + 1) * HALF]))
        v = (dot(parts[0], fwd[0:HALF, :]) + dot(parts[1], fwd[HALF:, :])).astype(BF)
        p12[:, :, (w - 1) * 256 : w * 256] = dot(pick[...], v).astype(BF).reshape(wide, 16, 256)
    send_sources(p12, s12, 0)

    lax.fori_loop(FIRST, groups, next12, 0)

    def arrived(landing, ws):
        some = landing.at[0, pl.ds(0, wide - 1)]
        pltpu.make_async_copy(some, some, p_recv.at[ws]).wait()
        pltpu.make_async_copy(landing.at[0, 0], landing.at[0, 0], own_sem.at[ws]).wait()

    def to_peer(landing, d, ws):
        return pltpu.make_async_remote_copy(
            src_ref=landing.at[n], dst_ref=landing.at[n], send_sem=b_send.at[ws, d], recv_sem=b_recv.at[ws, d],
            device_id={"narrow": y_peers[d] if d else other}, device_id_type=MESH)

    def across(landing, d, ws):
        part = y_froms[d] + core
        return pltpu.make_async_remote_copy(
            src_ref=landing.at[part], dst_ref=landing.at[part], send_sem=c_send.at[ws, d], recv_sem=c_recv.at[ws, d],
            device_id={"narrow": other}, device_id_type=MESH)

    def gather_start(landing, ws):
        arrived(landing, ws)
        for d in (1, 2, 3, 0):
            to_peer(landing, d, ws).start()

    def gather_across(landing, ws):
        for d in (1, 3, 2):
            to_peer(landing, d, ws).wait_recv()
            across(landing, d, ws).start()

    def gather_end(landing, ws):
        for d in range(4):
            to_peer(landing, d, ws).wait_send()
        to_peer(landing, 0, ws).wait_recv()
        for d in (1, 2, 3):
            across(landing, d, ws).wait()


    past_copy.wait()
    later = jnp.where(me > 0, 1.0, 0.0).astype(F32)

    def whiten_past(left, right, contract):
        return (dot(left, toep[HALF - PAST : HALF, :], contract) * later + dot(right, toep[HALF:, :])).astype(BF)

    for g in range(groups):
        block = past[:, g * 256 : (g + 1) * 256]
        past_source[pl.ds(g * 16, 16), 0:PAST] = dot(extract[...], block, NT).astype(BF)
    first = whiten_past(past_source[:, 0:PAST], vrec[:, 0:HALF], ((1,), (0,)))
    second = whiten(vrec[:, 0:HALF], vrec[:, HALF : 2 * HALF])
    v = (dot(first, fwd[0:HALF, :]) + dot(second, fwd[HALF:, :])).astype(BF)
    p0[...] = dot(pick[...], v).astype(BF).reshape(wide, 16, 256)
    send_sources(p0, s0, 1)

    def group0(gi, _):
        g = group_at(gi)
        h = past[:, pl.ds(pl.multiple_of(g * 256, 256), 256)]
        x = rec[pl.ds(g * 4, 4), :, 0 : 2 * HALF].reshape(256, 2 * HALF)

        def store(e, value):
            z0[g * 4 + e] = value

        transform(whiten_past(h, x[:, 0:HALF], TN), whiten(x[:, 0:HALF], x[:, HALF:]), store)
        send_group(z0, r0, g, 1)
        return 0

    onward()
    lax.fori_loop(0, groups, group0, 0)
    send_rest(z12, r12, 0, 1)
    send_rest(z0, r0, 1, 1)
    gather_start(s12, 0)

    def turn(s, j):
        st = dot(s.reshape(128, 256), perm[...], TN)
        start = pl.multiple_of(j * PITCH, 8)
        ss[0, pl.ds(start, 128), :] = st[0:128]
        ss[1, pl.ds(start, 128), :] = st[128:256]

    def turn12(d, _):
        for w in range(2):
            turn(s12[:, d, :, w * 256 : (w + 1) * 256], d * 2 + w)
        return 0

    def turn0(d, _):
        turn(s0[:, d], 64 + d)
        return 0

    gather_across(s12, 0)
    gather_start(s0, 1)
    gather_end(s12, 0)
    lax.fori_loop(0, wide, turn12, 0, unroll=2)
    gather_across(s0, 1)
    gather_end(s0, 1)
    lax.fori_loop(0, wide, turn0, 0, unroll=4)

    for ws, z in enumerate((z12, z0)):
        pltpu.make_async_copy(z.at[0], z.at[0], own_sem.at[2 + ws]).wait()

    def one_bin(f):
        left = rs[pl.ds(f, rows, stride=PITCH), :].T.astype(BF)
        turned = jnp.concatenate([left[64:128], -left[0:64]], 0)
        re = ss[0, pl.ds(f, rows, stride=PITCH), :].astype(BF)
        im = ss[1, pl.ds(f, rows, stride=PITCH), :].astype(BF)
        value = dot(left, re) + dot(turned, im)
        cross[pl.ds(pl.multiple_of(f * PITCH, 8), 128), :] = value * scale[0:1, :]

    def write(c):
        at = pl.ds(*CHUNKS[c])
        return pltpu.make_async_copy(turned_cross.at[:, :, at], out.at[:, :, at], out_sem.at[c])

    for c, (base, step) in enumerate(CHUNKS):
        for ws, landing in ((0, r12), (1, r0)):
            some = piece(landing, pl.ds(0, wide - 1), c)
            pltpu.make_async_copy(some, some, z_recv.at[ws, c]).wait()

        def widen(d, _, base=base, step=step):
            for j, part in ((2 * d, r12.at[d, 0]), (2 * d + 1, r12.at[d, 1]), (64 + d, r0.at[d])):
                rs[pl.ds(pl.multiple_of(j * PITCH + base, 8), step), :] = part[base : base + step, :].astype(F32)
            return 0

        lax.fori_loop(0, wide, widen, 0, unroll=4)

        def some_bins(i, _, base=base):
            for u in range(16):
                one_bin(base + i * 16 + u)
            return 0

        lax.fori_loop(0, step // 16, some_bins, 0)
        def regroup(i, _, base=base, step=step):
            for p in range(2):
                rows_of = cross[pl.ds(base * PITCH + p * 64 + i, step, stride=PITCH), :]
                turned_cross[i, p, base : base + step, :] = rows_of.astype(BF)
            return 0

        lax.fori_loop(0, 64, regroup, 0, unroll=8)
        write(c).start()

    pltpu.make_async_copy(relay, relay, onward_sem).wait()
    for ws, (z, p) in enumerate(((z12, p12), (z0, p0))):
        some = p.at[pl.ds(0, wide - 1)]
        pltpu.make_async_copy(some, some, p_send.at[ws]).wait()
        for c in range(len(CHUNKS)):
            some = piece(z, pl.ds(0, wide - 1), c)
            pltpu.make_async_copy(some, some, z_send.at[ws, c]).wait()
    for c in range(len(CHUNKS)):
        write(c).wait()


def lag_kernel(cross_hbm, lag_hbm, out_hbm, cross, lag, out, lag_sem, read_sem, write_sem):
    channels, parts = cross.shape[0], 4
    each = channels // parts

    def read(q):
        at = pl.ds(q * each, each)
        return pltpu.make_async_copy(cross_hbm.at[at], cross.at[at], read_sem.at[q])

    def write(q):
        at = pl.ds(q * each, each)
        return pltpu.make_async_copy(out.at[:, at], out_hbm.at[:, at], write_sem.at[q])

    table = pltpu.make_async_copy(lag_hbm, lag, lag_sem)
    table.start()
    for q in range(parts):
        read(q).start()
    table.wait()
    for q in range(parts):
        read(q).wait()
        for i in range(q * each, (q + 1) * each):
            x = cross[i].reshape(2 * BINS, 128)
            out[:, i] = dot(x, lag[...], TN).astype(BF).reshape(SLOTS, 32, LAGS)
        write(q).start()
    for q in range(parts):
        write(q).wait()


def on_device(records, taps, pair_sources, pair_counts):
    blocks, channels, _ = records.shape
    any_spec = pl.BlockSpec(memory_space=pl.ANY)
    smem = pl.BlockSpec(memory_space=pltpu.SMEM)
    forward = forward_table()
    extract = np.zeros((16, 256), ml_dtypes.bfloat16)
    extract[np.arange(16), np.arange(16) * 16] = 1
    repeat = np.zeros((512, 32), ml_dtypes.bfloat16)
    repeat[np.arange(512), np.arange(512) // 16] = 1
    perm = np.zeros((128, 128), ml_dtypes.bfloat16)
    for col in range(128):
        k, v = col // 32, col % 32
        perm[(v // 4) * 16 + k * 4 + v % 4, col] = 1
    shift = np.zeros((PAST, HALF), ml_dtypes.bfloat16)
    shift[np.arange(PAST), HALF - PAST + np.arange(PAST)] = 1
    dma = pltpu.SemaphoreType.DMA
    vm = lambda *shape, dtype=BF: pltpu.VMEM(shape, dtype)
    cross = pl.pallas_call(
        whole_kernel,
        out_shape=jax.ShapeDtypeStruct((channels, 2, BINS, 128), BF),
        in_specs=[smem] + [any_spec] * 9,
        out_specs=any_spec,
        scratch_shapes=[
            vm(1, TAPS, dtype=F32), vm(SLOTS, 32, dtype=jnp.int32), vm(512, 256), vm(256, 512), vm(16, 256),
            vm(512, 32), vm(128, 128), vm(PAST, HALF), vm(1, 1024, dtype=F32), vm(512, 256), vm(512, 128),
            vm(8, 128, dtype=F32),
            vm(blocks, channels, 1536), vm(PAST, blocks * channels), vm(PAST, blocks * channels), vm(128, HALF),
            vm(32, 2, 128, 128), vm(32, 128, 128), vm(32, 2, 128, 128), vm(32, 128, 128), vm(128, 1536),
            vm(32, 16, 512), vm(32, 16, 256), vm(8, 32, 16, 512), vm(8, 32, 16, 256),
            vm(96 * PITCH, 128, dtype=F32), vm(2, 96 * PITCH, 128, dtype=F32), vm(BINS * PITCH, 128, dtype=F32),
            vm(channels, 2, BINS, 128), vm(4, 2, CHUNKS[0][1], 128),
            dma((8,)), dma((9,)), dma((2,)), dma((2, len(CHUNKS))), dma((2, len(CHUNKS))), dma((2,)), dma((2,)), dma((4,)),
            dma((2, 4)), dma((2, 4)), dma((2, 4)), dma((2, 4)), dma, dma, dma((len(CHUNKS),))],
        compiler_params=pltpu.CompilerParams(collective_id=0, has_side_effects=True, vmem_limit_bytes=62 << 20),
        name="cross",
    )(pair_counts, records, taps.reshape(1, TAPS), pair_sources.T, jnp.asarray(forward), jnp.asarray(forward.T),
      jnp.asarray(extract), jnp.asarray(repeat), jnp.asarray(perm), jnp.asarray(shift))
    out = pl.pallas_call(
        lag_kernel,
        out_shape=jax.ShapeDtypeStruct((SLOTS, channels, 32, LAGS), BF),
        in_specs=[any_spec, any_spec],
        out_specs=any_spec,
        scratch_shapes=[
            vm(channels, 2, BINS, 128), vm(2 * BINS, LAGS), vm(SLOTS, channels, 32, LAGS), dma, dma((4,)), dma((4,))],
        compiler_params=pltpu.CompilerParams(vmem_limit_bytes=60 << 20),
        name="lags",
    )(cross, jnp.asarray(lag_table()))
    return out[None]


def solution(mesh):
    return jax.shard_map(
        on_device,
        mesh=mesh,
        in_specs=(P(None, "narrow", "wide"), P(), P(), P("wide")),
        out_specs=P("wide", None, "narrow", None, None),
        check_vma=False,
    )
```

```python
import math

import jax
import jax.numpy as jnp
import ml_dtypes
import numpy as np
from jax import lax
from jax.experimental import pallas as pl
from jax.experimental.pallas import tpu as pltpu
from jax.sharding import PartitionSpec as P

TAPS = 201
WLEN = 512
BINS = 128
F_LO = 4
LAGS = 256
SLOTS = 4
HALF = 256
PITCH = 136
PAST = 208
FIRST = 1
CHUNKS = ((0, 96), (96, 32))
MESH = pl.DeviceIdType.MESH
BF = jnp.bfloat16
F32 = jnp.float32


def forward_table():
    times = np.arange(WLEN)[:, None]
    bins = (F_LO + np.arange(BINS))[None, :]
    angle = ((times * bins) % WLEN).astype(np.float32) * np.float32(2.0 * math.pi / WLEN)
    scale = np.float32(1.0 / math.sqrt(WLEN))
    table = np.concatenate([np.cos(angle) * scale, -np.sin(angle) * scale], 1)
    return table.astype(ml_dtypes.bfloat16)


def lag_table():
    bins = (F_LO + np.arange(BINS))[:, None]
    lags = (np.arange(LAGS) - LAGS // 2)[None, :]
    angle = ((bins * lags) % WLEN).astype(np.float32) * np.float32(2.0 * math.pi / WLEN)
    scale = np.float32(1.0 / math.sqrt(BINS))
    table = np.concatenate([np.cos(angle) * scale, -np.sin(angle) * scale], 0)
    return table.astype(ml_dtypes.bfloat16)


def dot(a, b, contract=((1,), (0,))):
    return lax.dot_general(a, b, (contract, ((), ())), preferred_element_type=F32)


NT = ((1,), (1,))
TN = ((0,), (0,))


def fill_filter(taps, taps_row, toep):
    taps_row[...] = jnp.zeros_like(taps_row)
    taps_row[:, 0:TAPS] = taps[...].astype(BF).astype(F32)
    width = taps_row.shape[1]
    rolled = pltpu.roll(
        jnp.broadcast_to(taps_row[...], (2 * HALF, width)), width - HALF, 1, stride=1, stride_axis=0)
    toep[...] = rolled[:, :HALF].astype(BF)


def fill_picks(windows, pairs, counts, repeat, pick, scale):
    every = dot(repeat[...], pairs[...].astype(F32).astype(BF), NT)
    lane = lax.broadcasted_iota(jnp.int32, (512, SLOTS), 1)
    slot = lax.rem(lax.broadcasted_iota(jnp.int32, (512, SLOTS), 0) // 4, SLOTS)
    source = jnp.sum(jnp.where(lane == slot, every, 0.0), axis=1, keepdims=True)
    col = lax.broadcasted_iota(jnp.int32, (512, 128), 1)
    row = lax.broadcasted_iota(jnp.int32, (512, 128), 0)
    same = lax.rem(col, 4) == lax.rem(row, 4)
    pick[...] = jnp.where(same & ((col // 4).astype(F32) == source), 1.0, 0.0).astype(BF)
    slot = lax.broadcasted_iota(jnp.int32, (8, 128), 1) // 32
    scale[...] = jnp.where(slot < counts[0], 1.0 / math.sqrt(windows), 0.0).astype(F32)


def whole_kernel(
    counts, rec_hbm, taps_hbm, pairs_hbm, fwd_hbm, fwd_t_hbm, extract_hbm, repeat_hbm, perm_hbm, shift_hbm,
    out,
    taps, pairs, fwd, fwd_t, extract, repeat, perm, shift, taps_row, toep, pick, scale,
    rec, own_past, past, past_source, z12, z0, r12, r0, vrec, p12, p0, s12, s0, rs, ss, cross, turned_cross, relay,
    const_sem, load_sem, halo_sem, z_send, z_recv, p_send, p_recv, own_sem, b_send, b_recv, c_send, c_recv, relay_sem, onward_sem, out_sem,
):
    wide, groups, rows = 32, 8, 96
    me = lax.axis_index("wide")
    n = lax.axis_index("narrow")
    y, core = n // 2, lax.rem(n, 2)
    other = n + 1 - 2 * core

    consts = [
        pltpu.make_async_copy(a, b, const_sem.at[i])
        for i, (a, b) in enumerate((
            (taps_hbm, taps), (fwd_t_hbm, fwd_t), (shift_hbm, shift), (extract_hbm, extract), (pairs_hbm, pairs),
            (repeat_hbm, repeat), (fwd_hbm, fwd), (perm_hbm, perm)))
    ]

    def load(g):
        part = (pl.ds(g * 4, 4), slice(None), pl.ds(0, 1280))
        return pltpu.make_async_copy(rec_hbm.at[part], rec.at[part], load_sem.at[g])

    last = (slice(None), slice(None), pl.ds(1280, HALF))
    tails = pltpu.make_async_copy(rec_hbm.at[last], rec.at[last], load_sem.at[groups])

    for c in consts[0:2]:
        c.start()
    tails.start()
    x, z_at = me // 8, lax.rem(me, 8)

    def group_at(gi):
        return lax.rem(x + gi, 4) * 2 + lax.rem(z_at // 4 + 1 + gi // 4, 2)

    for gi in range(groups):
        load(group_at(gi)).start()
        if gi == 0:
            for c in consts[2:]:
                c.start()

    barrier = pltpu.get_barrier_semaphore()

    def greet(o, _):
        pl.semaphore_signal(barrier, inc=1, device_id={"wide": lax.rem(me + o, wide)}, device_id_type=MESH)
        return 0

    lax.fori_loop(1, wide, greet, 0)
    y_peers = [lax.rem(y + d, 4) * 2 + core for d in range(4)]
    y_froms = [lax.rem(y + 4 - d, 4) * 2 for d in range(4)]
    for peer in y_peers[1:] + [other]:
        pl.semaphore_signal(barrier, inc=1, device_id={"narrow": peer}, device_id_type=MESH)

    for c in consts[0:2]:
        c.wait()
    fill_filter(taps, taps_row, toep)

    def whiten(left, right):
        return (dot(left, toep[0:HALF, :]) + dot(right, toep[HALF:, :])).astype(BF)

    def send_sources(picked, landing, ws):
        def one(o, _):
            dst = lax.rem(me + o, wide)
            pltpu.make_async_remote_copy(
                src_ref=picked.at[dst], dst_ref=landing.at[n, me], send_sem=p_send.at[ws], recv_sem=p_recv.at[ws],
                device_id={"wide": dst}, device_id_type=MESH).start()
            return 0

        lax.fori_loop(1, wide, one, 0)
        pltpu.make_async_copy(picked.at[me], landing.at[n, me], own_sem.at[ws]).start()

    left_half = lax.broadcasted_iota(jnp.int32, (128, 128), 1) < 64

    def transform(first, second, store):
        a = dot(fwd_t[:, 0:HALF], first, NT) + dot(fwd_t[:, HALF:], second, NT)
        for t in range(2):
            re, im = a[0:128, t * 128 : (t + 1) * 128], a[128:256, t * 128 : (t + 1) * 128]
            store(2 * t, jnp.where(left_half, re, pltpu.roll(im, 64, 1)).astype(BF))
            store(2 * t + 1, jnp.where(left_half, pltpu.roll(re, 64, 1), im).astype(BF))

    def piece(ref, lead, c):
        at = pl.ds(*CHUNKS[c])
        return ref.at[lead, :, at] if len(ref.shape) == 4 else ref.at[lead, at]

    def send_piece(z, landing, dst, ws, c):
        pltpu.make_async_remote_copy(
            src_ref=piece(z, dst, c), dst_ref=piece(landing, me, c),
            send_sem=z_send.at[ws, c], recv_sem=z_recv.at[ws, c],
            device_id={"wide": dst}, device_id_type=MESH).start()

    half_way, relay_to = lax.rem(z_at + 4, 8), x * 8 + lax.rem(z_at + 6, 8)

    def send_group(z, landing, g, ws):
        for e in range(4):
            dst = g * 4 + e
            far = (lax.rem(dst, 8) == half_way) if ws == 0 else False

            @pl.when((dst != me) & jnp.logical_not(far))
            def _():
                send_piece(z, landing, dst, ws, 0)

            if ws == 0:

                @pl.when(far)
                def _():
                    pltpu.make_async_remote_copy(
                        src_ref=piece(z, dst, 0), dst_ref=relay.at[lax.rem(dst // 8 + 4 - x, 4)],
                        send_sem=z_send.at[ws, 0], recv_sem=relay_sem,
                        device_id={"wide": relay_to}, device_id_type=MESH).start()

            @pl.when(dst == me)
            def _():
                pltpu.make_async_copy(z.at[dst], landing.at[me], own_sem.at[2 + ws]).start()

    def onward():
        pltpu.make_async_copy(relay, relay, relay_sem).wait()
        origin = x * 8 + lax.rem(z_at + 2, 8)
        for d in range(4):
            pltpu.make_async_remote_copy(
                src_ref=relay.at[d], dst_ref=piece(r12, origin, 0),
                send_sem=onward_sem, recv_sem=z_recv.at[0, 0],
                device_id={"wide": lax.rem(x + d, 4) * 8 + lax.rem(z_at + 6, 8)}, device_id_type=MESH).start()

    def send_rest(z, landing, ws, c):
        def one(o, _):
            send_piece(z, landing, lax.rem(me + o, wide), ws, c)
            return 0

        lax.fori_loop(1, wide, one, 0)

    def group12(gi, _):
        g = group_at(gi)
        x = rec[pl.ds(g * 4, 4)].reshape(256, 1536)
        for w in (1, 2):
            parts = []
            for h in (2 * w, 2 * w + 1):
                parts.append(whiten(x[:, (h - 1) * HALF : h * HALF], x[:, h * HALF : (h + 1) * HALF]))

            def store(e, value, w=w):
                z12[g * 4 + e, w - 1] = value

            transform(parts[0], parts[1], store)
        return 0

    def send12(gi, _):
        send_group(z12, r12, group_at(gi), 0)
        return 0

    def next12(gi, _):
        group12(gi, 0)
        return send12(gi, 0)

    def first12(gi, _):
        load(group_at(gi)).wait()
        return group12(gi, 0)

    tails.wait()
    lax.fori_loop(0, FIRST, first12, 0)

    pl.semaphore_wait(barrier, wide - 1 + 4)
    lax.fori_loop(0, FIRST, send12, 0)

    for c in consts[2:]:
        c.wait()
    for g in range(groups):
        tail = rec[pl.ds(g * 4, 4), :, 1280:].reshape(256, HALF)
        own_past[:, g * 256 : (g + 1) * 256] = dot(shift[...], tail, NT).astype(BF)
    past_copy = pltpu.make_async_remote_copy(
        src_ref=own_past, dst_ref=past, send_sem=halo_sem.at[0], recv_sem=halo_sem.at[1],
        device_id={"wide": lax.rem(me + 1, wide)}, device_id_type=MESH)
    past_copy.start()
    fill_picks(rows, pairs, counts, repeat, pick, scale)

    for gi in range(FIRST, groups):
        load(group_at(gi)).wait()
    for g in range(groups):
        block = rec[pl.ds(g * 4, 4)].reshape(256, 1536)
        vrec[pl.ds(g * 16, 16), :] = dot(extract[...], block).astype(BF)
    for w in (1, 2):
        parts = []
        for h in (2 * w, 2 * w + 1):
            parts.append(whiten(vrec[:, (h - 1) * HALF : h * HALF], vrec[:, h * HALF : (h + 1) * HALF]))
        v = (dot(parts[0], fwd[0:HALF, :]) + dot(parts[1], fwd[HALF:, :])).astype(BF)
        p12[:, :, (w - 1) * 256 : w * 256] = dot(pick[...], v).astype(BF).reshape(wide, 16, 256)
    send_sources(p12, s12, 0)

    lax.fori_loop(FIRST, groups, next12, 0)

    def arrived(landing, ws):
        some = landing.at[0, pl.ds(0, wide - 1)]
        pltpu.make_async_copy(some, some, p_recv.at[ws]).wait()
        pltpu.make_async_copy(landing.at[0, 0], landing.at[0, 0], own_sem.at[ws]).wait()

    def to_peer(landing, d, ws):
        return pltpu.make_async_remote_copy(
            src_ref=landing.at[n], dst_ref=landing.at[n], send_sem=b_send.at[ws, d], recv_sem=b_recv.at[ws, d],
            device_id={"narrow": y_peers[d] if d else other}, device_id_type=MESH)

    def across(landing, d, ws):
        part = y_froms[d] + core
        return pltpu.make_async_remote_copy(
            src_ref=landing.at[part], dst_ref=landing.at[part], send_sem=c_send.at[ws, d], recv_sem=c_recv.at[ws, d],
            device_id={"narrow": other}, device_id_type=MESH)

    def gather_start(landing, ws):
        arrived(landing, ws)
        for d in (1, 2, 3, 0):
            to_peer(landing, d, ws).start()

    def gather_across(landing, ws):
        for d in (1, 3, 2):
            to_peer(landing, d, ws).wait_recv()
            across(landing, d, ws).start()

    def gather_end(landing, ws):
        for d in range(4):
            to_peer(landing, d, ws).wait_send()
        to_peer(landing, 0, ws).wait_recv()
        for d in (1, 2, 3):
            across(landing, d, ws).wait()


    past_copy.wait()
    later = jnp.where(me > 0, 1.0, 0.0).astype(F32)

    def whiten_past(left, right, contract):
        return (dot(left, toep[HALF - PAST : HALF, :], contract) * later + dot(right, toep[HALF:, :])).astype(BF)

    for g in range(groups):
        block = past[:, g * 256 : (g + 1) * 256]
        past_source[pl.ds(g * 16, 16), 0:PAST] = dot(extract[...], block, NT).astype(BF)
    first = whiten_past(past_source[:, 0:PAST], vrec[:, 0:HALF], ((1,), (0,)))
    second = whiten(vrec[:, 0:HALF], vrec[:, HALF : 2 * HALF])
    v = (dot(first, fwd[0:HALF, :]) + dot(second, fwd[HALF:, :])).astype(BF)
    p0[...] = dot(pick[...], v).astype(BF).reshape(wide, 16, 256)
    send_sources(p0, s0, 1)

    def group0(gi, _):
        g = group_at(gi)
        h = past[:, pl.ds(pl.multiple_of(g * 256, 256), 256)]
        x = rec[pl.ds(g * 4, 4), :, 0 : 2 * HALF].reshape(256, 2 * HALF)

        def store(e, value):
            z0[g * 4 + e] = value

        transform(whiten_past(h, x[:, 0:HALF], TN), whiten(x[:, 0:HALF], x[:, HALF:]), store)
        send_group(z0, r0, g, 1)
        return 0

    onward()
    lax.fori_loop(0, groups, group0, 0)
    send_rest(z12, r12, 0, 1)
    send_rest(z0, r0, 1, 1)
    gather_start(s12, 0)

    def turn(s, j):
        st = dot(s.reshape(128, 256), perm[...], TN)
        start = pl.multiple_of(j * PITCH, 8)
        ss[0, pl.ds(start, 128), :] = st[0:128]
        ss[1, pl.ds(start, 128), :] = st[128:256]

    def turn12(d, _):
        for w in range(2):
            turn(s12[:, d, :, w * 256 : (w + 1) * 256], d * 2 + w)
        return 0

    def turn0(d, _):
        turn(s0[:, d], 64 + d)
        return 0

    gather_across(s12, 0)
    gather_start(s0, 1)
    gather_end(s12, 0)
    lax.fori_loop(0, wide, turn12, 0, unroll=2)
    gather_across(s0, 1)
    gather_end(s0, 1)
    lax.fori_loop(0, wide, turn0, 0, unroll=4)

    for ws, z in enumerate((z12, z0)):
        pltpu.make_async_copy(z.at[0], z.at[0], own_sem.at[2 + ws]).wait()

    def one_bin(f):
        left = rs[pl.ds(f, rows, stride=PITCH), :].T.astype(BF)
        turned = jnp.concatenate([left[64:128], -left[0:64]], 0)
        re = ss[0, pl.ds(f, rows, stride=PITCH), :].astype(BF)
        im = ss[1, pl.ds(f, rows, stride=PITCH), :].astype(BF)
        value = dot(left, re) + dot(turned, im)
        cross[pl.ds(pl.multiple_of(f * PITCH, 8), 128), :] = value * scale[0:1, :]

    def write(c):
        at = pl.ds(*CHUNKS[c])
        return pltpu.make_async_copy(turned_cross.at[:, :, at], out.at[:, :, at], out_sem.at[c])

    for c, (base, step) in enumerate(CHUNKS):
        for ws, landing in ((0, r12), (1, r0)):
            some = piece(landing, pl.ds(0, wide - 1), c)
            pltpu.make_async_copy(some, some, z_recv.at[ws, c]).wait()

        def widen(d, _, base=base, step=step):
            for j, part in ((2 * d, r12.at[d, 0]), (2 * d + 1, r12.at[d, 1]), (64 + d, r0.at[d])):
                rs[pl.ds(pl.multiple_of(j * PITCH + base, 8), step), :] = part[base : base + step, :].astype(F32)
            return 0

        lax.fori_loop(0, wide, widen, 0, unroll=4)

        def some_bins(i, _, base=base):
            for u in range(16):
                one_bin(base + i * 16 + u)
            return 0

        lax.fori_loop(0, step // 16, some_bins, 0)
        def regroup(i, _, base=base, step=step):
            for p in range(2):
                rows_of = cross[pl.ds(base * PITCH + p * 64 + i, step, stride=PITCH), :]
                turned_cross[i, p, base : base + step, :] = rows_of.astype(BF)
            return 0

        lax.fori_loop(0, 64, regroup, 0, unroll=8)
        write(c).start()

    pltpu.make_async_copy(relay, relay, onward_sem).wait()
    for ws, (z, p) in enumerate(((z12, p12), (z0, p0))):
        some = p.at[pl.ds(0, wide - 1)]
        pltpu.make_async_copy(some, some, p_send.at[ws]).wait()
        for c in range(len(CHUNKS)):
            some = piece(z, pl.ds(0, wide - 1), c)
            pltpu.make_async_copy(some, some, z_send.at[ws, c]).wait()
    for c in range(len(CHUNKS)):
        write(c).wait()


def lag_kernel(cross_hbm, lag_hbm, out_hbm, cross, lag, out, lag_sem, read_sem, write_sem):
    channels, parts = cross.shape[0], 4
    each = channels // parts

    def read(q):
        at = pl.ds(q * each, each)
        return pltpu.make_async_copy(cross_hbm.at[at], cross.at[at], read_sem.at[q])

    def write(q):
        at = pl.ds(q * each, each)
        return pltpu.make_async_copy(out.at[:, at], out_hbm.at[:, at], write_sem.at[q])

    table = pltpu.make_async_copy(lag_hbm, lag, lag_sem)
    table.start()
    for q in range(parts):
        read(q).start()
    table.wait()
    for q in range(parts):
        read(q).wait()
        for i in range(q * each, (q + 1) * each):
            x = cross[i].reshape(2 * BINS, 128)
            out[:, i] = dot(x, lag[...], TN).astype(BF).reshape(SLOTS, 32, LAGS)
        write(q).start()
    for q in range(parts):
        write(q).wait()


def on_device(records, taps, pair_sources, pair_counts):
    blocks, channels, _ = records.shape
    any_spec = pl.BlockSpec(memory_space=pl.ANY)
    smem = pl.BlockSpec(memory_space=pltpu.SMEM)
    forward = forward_table()
    extract = np.zeros((16, 256), ml_dtypes.bfloat16)
    extract[np.arange(16), np.arange(16) * 16] = 1
    repeat = np.zeros((512, 32), ml_dtypes.bfloat16)
    repeat[np.arange(512), np.arange(512) // 16] = 1
    perm = np.zeros((128, 128), ml_dtypes.bfloat16)
    for col in range(128):
        k, v = col // 32, col % 32
        perm[(v // 4) * 16 + k * 4 + v % 4, col] = 1
    shift = np.zeros((PAST, HALF), ml_dtypes.bfloat16)
    shift[np.arange(PAST), HALF - PAST + np.arange(PAST)] = 1
    dma = pltpu.SemaphoreType.DMA
    vm = lambda *shape, dtype=BF: pltpu.VMEM(shape, dtype)
    cross = pl.pallas_call(
        whole_kernel,
        out_shape=jax.ShapeDtypeStruct((channels, 2, BINS, 128), BF),
        in_specs=[smem] + [any_spec] * 9,
        out_specs=any_spec,
        scratch_shapes=[
            vm(1, TAPS, dtype=F32), vm(SLOTS, 32, dtype=jnp.int32), vm(512, 256), vm(256, 512), vm(16, 256),
            vm(512, 32), vm(128, 128), vm(PAST, HALF), vm(1, 1024, dtype=F32), vm(512, 256), vm(512, 128),
            vm(8, 128, dtype=F32),
            vm(blocks, channels, 1536), vm(PAST, blocks * channels), vm(PAST, blocks * channels), vm(128, HALF),
            vm(32, 2, 128, 128), vm(32, 128, 128), vm(32, 2, 128, 128), vm(32, 128, 128), vm(128, 1536),
            vm(32, 16, 512), vm(32, 16, 256), vm(8, 32, 16, 512), vm(8, 32, 16, 256),
            vm(97 * PITCH, 128, dtype=F32), vm(2, 97 * PITCH, 128, dtype=F32), vm((BINS + 1) * PITCH, 128, dtype=F32),
            vm(channels, 2, BINS, 128), vm(4, 2, CHUNKS[0][1], 128),
            dma((8,)), dma((9,)), dma((2,)), dma((2, len(CHUNKS))), dma((2, len(CHUNKS))), dma((2,)), dma((2,)), dma((4,)),
            dma((2, 4)), dma((2, 4)), dma((2, 4)), dma((2, 4)), dma, dma, dma((len(CHUNKS),))],
        compiler_params=pltpu.CompilerParams(collective_id=0, has_side_effects=True, vmem_limit_bytes=62 << 20),
        name="cross",
    )(pair_counts, records, taps.reshape(1, TAPS), pair_sources.T, jnp.asarray(forward), jnp.asarray(forward.T),
      jnp.asarray(extract), jnp.asarray(repeat), jnp.asarray(perm), jnp.asarray(shift))
    out = pl.pallas_call(
        lag_kernel,
        out_shape=jax.ShapeDtypeStruct((SLOTS, channels, 32, LAGS), BF),
        in_specs=[any_spec, any_spec],
        out_specs=any_spec,
        scratch_shapes=[
            vm(channels, 2, BINS, 128), vm(2 * BINS, LAGS), vm(SLOTS, channels, 32, LAGS), dma, dma((4,)), dma((4,))],
        compiler_params=pltpu.CompilerParams(vmem_limit_bytes=60 << 20),
        name="lags",
    )(cross, jnp.asarray(lag_table()))
    return out[None]


def solution(mesh):
    return jax.shard_map(
        on_device,
        mesh=mesh,
        in_specs=(P(None, "narrow", "wide"), P(), P(), P("wide")),
        out_specs=P("wide", None, "narrow", None, None),
        check_vma=False,
    )
```

```python
import math

import jax
import jax.numpy as jnp
import ml_dtypes
import numpy as np
from jax import lax
from jax.experimental import pallas as pl
from jax.experimental.pallas import tpu as pltpu
from jax.sharding import PartitionSpec as P

TAPS = 201
WLEN = 512
BINS = 128
F_LO = 4
LAGS = 256
SLOTS = 4
HALF = 256
PITCH = 136
PAST = 208
FIRST = 1
CHUNKS = ((0, 96), (96, 32))
MESH = pl.DeviceIdType.MESH
BF = jnp.bfloat16
F32 = jnp.float32


def forward_table():
    times = np.arange(WLEN)[:, None]
    bins = (F_LO + np.arange(BINS))[None, :]
    angle = ((times * bins) % WLEN).astype(np.float32) * np.float32(2.0 * math.pi / WLEN)
    scale = np.float32(1.0 / math.sqrt(WLEN))
    table = np.concatenate([np.cos(angle) * scale, -np.sin(angle) * scale], 1)
    return table.astype(ml_dtypes.bfloat16)


def lag_table():
    bins = (F_LO + np.arange(BINS))[:, None]
    lags = (np.arange(LAGS) - LAGS // 2)[None, :]
    angle = ((bins * lags) % WLEN).astype(np.float32) * np.float32(2.0 * math.pi / WLEN)
    scale = np.float32(1.0 / math.sqrt(BINS))
    table = np.concatenate([np.cos(angle) * scale, -np.sin(angle) * scale], 0)
    return table.astype(ml_dtypes.bfloat16)


def dot(a, b, contract=((1,), (0,))):
    return lax.dot_general(a, b, (contract, ((), ())), preferred_element_type=F32)


NT = ((1,), (1,))
TN = ((0,), (0,))


def fill_filter(taps, taps_row, toep):
    taps_row[...] = jnp.zeros_like(taps_row)
    taps_row[:, 0:TAPS] = taps[...].astype(BF).astype(F32)
    width = taps_row.shape[1]
    rolled = pltpu.roll(
        jnp.broadcast_to(taps_row[...], (2 * HALF, width)), width - HALF, 1, stride=1, stride_axis=0)
    toep[...] = rolled[:, :HALF].astype(BF)


def fill_picks(windows, pairs, counts, repeat, pick, scale):
    every = dot(repeat[...], pairs[...].astype(F32).astype(BF), NT)
    lane = lax.broadcasted_iota(jnp.int32, (512, SLOTS), 1)
    slot = lax.rem(lax.broadcasted_iota(jnp.int32, (512, SLOTS), 0) // 4, SLOTS)
    source = jnp.sum(jnp.where(lane == slot, every, 0.0), axis=1, keepdims=True)
    col = lax.broadcasted_iota(jnp.int32, (512, 128), 1)
    row = lax.broadcasted_iota(jnp.int32, (512, 128), 0)
    same = lax.rem(col, 4) == lax.rem(row, 4)
    pick[...] = jnp.where(same & ((col // 4).astype(F32) == source), 1.0, 0.0).astype(BF)
    slot = lax.broadcasted_iota(jnp.int32, (8, 128), 1) // 32
    scale[...] = jnp.where(slot < counts[0], 1.0 / math.sqrt(windows), 0.0).astype(F32)


def whole_kernel(
    counts, rec_hbm, taps_hbm, pairs_hbm, fwd_hbm, fwd_t_hbm, extract_hbm, repeat_hbm, perm_hbm, shift_hbm,
    out,
    taps, pairs, fwd, fwd_t, extract, repeat, perm, shift, taps_row, toep, pick, scale,
    rec, own_past, past, past_source, z12, z0, r12, r0, vrec, p12, p0, s12, s0, rs, ss, cross, turned_cross, relay,
    const_sem, load_sem, halo_sem, z_send, z_recv, p_send, p_recv, own_sem, b_send, b_recv, c_send, c_recv, relay_sem, onward_sem, out_sem,
):
    wide, groups, rows = 32, 8, 96
    me = lax.axis_index("wide")
    n = lax.axis_index("narrow")
    y, core = n // 2, lax.rem(n, 2)
    other = n + 1 - 2 * core

    consts = [
        pltpu.make_async_copy(a, b, const_sem.at[i])
        for i, (a, b) in enumerate((
            (taps_hbm, taps), (fwd_t_hbm, fwd_t), (shift_hbm, shift), (extract_hbm, extract), (pairs_hbm, pairs),
            (repeat_hbm, repeat), (fwd_hbm, fwd), (perm_hbm, perm)))
    ]

    def load(g):
        part = (pl.ds(g * 4, 4), slice(None), pl.ds(0, 1280))
        return pltpu.make_async_copy(rec_hbm.at[part], rec.at[part], load_sem.at[g])

    last = (slice(None), slice(None), pl.ds(1280, HALF))
    tails = pltpu.make_async_copy(rec_hbm.at[last], rec.at[last], load_sem.at[groups])

    for c in consts[0:2]:
        c.start()
    tails.start()
    x, z_at = me // 8, lax.rem(me, 8)

    def group_at(gi):
        return lax.rem(x + gi, 4) * 2 + lax.rem(z_at // 4 + 1 + gi // 4, 2)

    for gi in range(groups):
        load(group_at(gi)).start()
        if gi == 0:
            for c in consts[2:]:
                c.start()

    barrier = pltpu.get_barrier_semaphore()

    def greet(o, _):
        pl.semaphore_signal(barrier, inc=1, device_id={"wide": lax.rem(me + o, wide)}, device_id_type=MESH)
        return 0

    lax.fori_loop(1, wide, greet, 0)
    y_peers = [lax.rem(y + d, 4) * 2 + core for d in range(4)]
    y_froms = [lax.rem(y + 4 - d, 4) * 2 for d in range(4)]
    for peer in y_peers[1:] + [other]:
        pl.semaphore_signal(barrier, inc=1, device_id={"narrow": peer}, device_id_type=MESH)

    for c in consts[0:2]:
        c.wait()
    fill_filter(taps, taps_row, toep)

    def whiten(left, right):
        return (dot(left, toep[0:HALF, :]) + dot(right, toep[HALF:, :])).astype(BF)

    def send_sources(picked, landing, ws):
        def one(o, _):
            dst = lax.rem(me + o, wide)
            pltpu.make_async_remote_copy(
                src_ref=picked.at[dst], dst_ref=landing.at[n, me], send_sem=p_send.at[ws], recv_sem=p_recv.at[ws],
                device_id={"wide": dst}, device_id_type=MESH).start()
            return 0

        lax.fori_loop(1, wide, one, 0)
        pltpu.make_async_copy(picked.at[me], landing.at[n, me], own_sem.at[ws]).start()

    left_half = lax.broadcasted_iota(jnp.int32, (128, 128), 1) < 64

    def transform(first, second, store):
        a = dot(fwd_t[:, 0:HALF], first, NT) + dot(fwd_t[:, HALF:], second, NT)
        for t in range(2):
            re, im = a[0:128, t * 128 : (t + 1) * 128], a[128:256, t * 128 : (t + 1) * 128]
            store(2 * t, jnp.where(left_half, re, pltpu.roll(im, 64, 1)).astype(BF))
            store(2 * t + 1, jnp.where(left_half, pltpu.roll(re, 64, 1), im).astype(BF))

    def piece(ref, lead, c):
        at = pl.ds(*CHUNKS[c])
        return ref.at[lead, :, at] if len(ref.shape) == 4 else ref.at[lead, at]

    def send_piece(z, landing, dst, ws, c):
        pltpu.make_async_remote_copy(
            src_ref=piece(z, dst, c), dst_ref=piece(landing, me, c),
            send_sem=z_send.at[ws, c], recv_sem=z_recv.at[ws, c],
            device_id={"wide": dst}, device_id_type=MESH).start()

    half_way, relay_to = lax.rem(z_at + 4, 8), x * 8 + lax.rem(z_at + 6, 8)

    def send_group(z, landing, g, ws):
        for e in range(4):
            dst = g * 4 + e
            far = (lax.rem(dst, 8) == half_way) if ws == 0 else False

            @pl.when((dst != me) & jnp.logical_not(far))
            def _():
                send_piece(z, landing, dst, ws, 0)

            if ws == 0:

                @pl.when(far)
                def _():
                    pltpu.make_async_remote_copy(
                        src_ref=piece(z, dst, 0), dst_ref=relay.at[lax.rem(dst // 8 + 4 - x, 4)],
                        send_sem=z_send.at[ws, 0], recv_sem=relay_sem,
                        device_id={"wide": relay_to}, device_id_type=MESH).start()

            @pl.when(dst == me)
            def _():
                pltpu.make_async_copy(z.at[dst], landing.at[me], own_sem.at[2 + ws]).start()

    def onward():
        pltpu.make_async_copy(relay, relay, relay_sem).wait()
        origin = x * 8 + lax.rem(z_at + 2, 8)
        for d in range(4):
            pltpu.make_async_remote_copy(
                src_ref=relay.at[d], dst_ref=piece(r12, origin, 0),
                send_sem=onward_sem, recv_sem=z_recv.at[0, 0],
                device_id={"wide": lax.rem(x + d, 4) * 8 + lax.rem(z_at + 6, 8)}, device_id_type=MESH).start()

    def send_rest(z, landing, ws, c):
        def one(o, _):
            send_piece(z, landing, lax.rem(me + o, wide), ws, c)
            return 0

        lax.fori_loop(1, wide, one, 0)

    def group12(gi, _):
        g = group_at(gi)
        x = rec[pl.ds(g * 4, 4)].reshape(256, 1536)
        for w in (1, 2):
            parts = []
            for h in (2 * w, 2 * w + 1):
                parts.append(whiten(x[:, (h - 1) * HALF : h * HALF], x[:, h * HALF : (h + 1) * HALF]))

            def store(e, value, w=w):
                z12[g * 4 + e, w - 1] = value

            transform(parts[0], parts[1], store)
        return 0

    def send12(gi, _):
        send_group(z12, r12, group_at(gi), 0)
        return 0

    def next12(gi, _):
        group12(gi, 0)
        return send12(gi, 0)

    def first12(gi, _):
        load(group_at(gi)).wait()
        return group12(gi, 0)

    tails.wait()
    lax.fori_loop(0, FIRST, first12, 0)

    pl.semaphore_wait(barrier, wide - 1 + 4)
    lax.fori_loop(0, FIRST, send12, 0)

    for c in consts[2:]:
        c.wait()
    for g in range(groups):
        tail = rec[pl.ds(g * 4, 4), :, 1280:].reshape(256, HALF)
        own_past[:, g * 256 : (g + 1) * 256] = dot(shift[...], tail, NT).astype(BF)
    past_copy = pltpu.make_async_remote_copy(
        src_ref=own_past, dst_ref=past, send_sem=halo_sem.at[0], recv_sem=halo_sem.at[1],
        device_id={"wide": lax.rem(me + 1, wide)}, device_id_type=MESH)
    past_copy.start()
    fill_picks(rows, pairs, counts, repeat, pick, scale)

    for gi in range(FIRST, groups):
        load(group_at(gi)).wait()
    for g in range(groups):
        block = rec[pl.ds(g * 4, 4)].reshape(256, 1536)
        vrec[pl.ds(g * 16, 16), :] = dot(extract[...], block).astype(BF)
    for w in (1, 2):
        parts = []
        for h in (2 * w, 2 * w + 1):
            parts.append(whiten(vrec[:, (h - 1) * HALF : h * HALF], vrec[:, h * HALF : (h + 1) * HALF]))
        v = (dot(parts[0], fwd[0:HALF, :]) + dot(parts[1], fwd[HALF:, :])).astype(BF)
        p12[:, :, (w - 1) * 256 : w * 256] = dot(pick[...], v).astype(BF).reshape(wide, 16, 256)
    send_sources(p12, s12, 0)

    lax.fori_loop(FIRST, 6, next12, 0)
    lax.fori_loop(6, groups, group12, 0)

    def arrived(landing, ws):
        some = landing.at[0, pl.ds(0, wide - 1)]
        pltpu.make_async_copy(some, some, p_recv.at[ws]).wait()
        pltpu.make_async_copy(landing.at[0, 0], landing.at[0, 0], own_sem.at[ws]).wait()

    def to_peer(landing, d, ws):
        return pltpu.make_async_remote_copy(
            src_ref=landing.at[n], dst_ref=landing.at[n], send_sem=b_send.at[ws, d], recv_sem=b_recv.at[ws, d],
            device_id={"narrow": y_peers[d] if d else other}, device_id_type=MESH)

    def across(landing, d, ws):
        part = y_froms[d] + core
        return pltpu.make_async_remote_copy(
            src_ref=landing.at[part], dst_ref=landing.at[part], send_sem=c_send.at[ws, d], recv_sem=c_recv.at[ws, d],
            device_id={"narrow": other}, device_id_type=MESH)

    def gather_start(landing, ws):
        arrived(landing, ws)
        for d in (1, 2, 3, 0):
            to_peer(landing, d, ws).start()

    def gather_across(landing, ws):
        for d in (1, 3, 2):
            to_peer(landing, d, ws).wait_recv()
            across(landing, d, ws).start()

    def gather_end(landing, ws):
        for d in range(4):
            to_peer(landing, d, ws).wait_send()
        to_peer(landing, 0, ws).wait_recv()
        for d in (1, 2, 3):
            across(landing, d, ws).wait()


    past_copy.wait()
    later = jnp.where(me > 0, 1.0, 0.0).astype(F32)

    def whiten_past(left, right, contract):
        return (dot(left, toep[HALF - PAST : HALF, :], contract) * later + dot(right, toep[HALF:, :])).astype(BF)

    for g in range(groups):
        block = past[:, g * 256 : (g + 1) * 256]
        past_source[pl.ds(g * 16, 16), 0:PAST] = dot(extract[...], block, NT).astype(BF)
    first = whiten_past(past_source[:, 0:PAST], vrec[:, 0:HALF], ((1,), (0,)))
    second = whiten(vrec[:, 0:HALF], vrec[:, HALF : 2 * HALF])
    v = (dot(first, fwd[0:HALF, :]) + dot(second, fwd[HALF:, :])).astype(BF)
    p0[...] = dot(pick[...], v).astype(BF).reshape(wide, 16, 256)
    send_sources(p0, s0, 1)
    lax.fori_loop(6, groups, send12, 0)

    def group0(gi, _):
        g = group_at(gi)
        h = past[:, pl.ds(pl.multiple_of(g * 256, 256), 256)]
        x = rec[pl.ds(g * 4, 4), :, 0 : 2 * HALF].reshape(256, 2 * HALF)

        def store(e, value):
            z0[g * 4 + e] = value

        transform(whiten_past(h, x[:, 0:HALF], TN), whiten(x[:, 0:HALF], x[:, HALF:]), store)
        send_group(z0, r0, g, 1)
        return 0

    onward()
    lax.fori_loop(0, groups, group0, 0)
    send_rest(z12, r12, 0, 1)
    send_rest(z0, r0, 1, 1)
    gather_start(s12, 0)

    def turn(s, j):
        st = dot(s.reshape(128, 256), perm[...], TN)
        start = pl.multiple_of(j * PITCH, 8)
        ss[0, pl.ds(start, 128), :] = st[0:128]
        ss[1, pl.ds(start, 128), :] = st[128:256]

    def turn12(d, _):
        for w in range(2):
            turn(s12[:, d, :, w * 256 : (w + 1) * 256], d * 2 + w)
        return 0

    def turn0(d, _):
        turn(s0[:, d], 64 + d)
        return 0

    gather_across(s12, 0)
    gather_start(s0, 1)
    gather_end(s12, 0)
    lax.fori_loop(0, wide, turn12, 0, unroll=2)
    gather_across(s0, 1)
    gather_end(s0, 1)
    lax.fori_loop(0, wide, turn0, 0, unroll=4)

    for ws, z in enumerate((z12, z0)):
        pltpu.make_async_copy(z.at[0], z.at[0], own_sem.at[2 + ws]).wait()

    def one_bin(f):
        left = rs[pl.ds(f, rows, stride=PITCH), :].T.astype(BF)
        turned = jnp.concatenate([left[64:128], -left[0:64]], 0)
        re = ss[0, pl.ds(f, rows, stride=PITCH), :].astype(BF)
        im = ss[1, pl.ds(f, rows, stride=PITCH), :].astype(BF)
        value = dot(left, re) + dot(turned, im)
        cross[pl.ds(pl.multiple_of(f * PITCH, 8), 128), :] = value * scale[0:1, :]

    def write(c):
        at = pl.ds(*CHUNKS[c])
        return pltpu.make_async_copy(turned_cross.at[:, :, at], out.at[:, :, at], out_sem.at[c])

    for c, (base, step) in enumerate(CHUNKS):
        for ws, landing in ((0, r12), (1, r0)):
            some = piece(landing, pl.ds(0, wide - 1), c)
            pltpu.make_async_copy(some, some, z_recv.at[ws, c]).wait()

        def widen(d, _, base=base, step=step):
            for j, part in ((2 * d, r12.at[d, 0]), (2 * d + 1, r12.at[d, 1]), (64 + d, r0.at[d])):
                rs[pl.ds(pl.multiple_of(j * PITCH + base, 8), step), :] = part[base : base + step, :].astype(F32)
            return 0

        lax.fori_loop(0, wide, widen, 0, unroll=4)

        def some_bins(i, _, base=base):
            for u in range(16):
                one_bin(base + i * 16 + u)
            return 0

        lax.fori_loop(0, step // 16, some_bins, 0)
        def regroup(i, _, base=base, step=step):
            for p in range(2):
                rows_of = cross[pl.ds(base * PITCH + p * 64 + i, step, stride=PITCH), :]
                turned_cross[i, p, base : base + step, :] = rows_of.astype(BF)
            return 0

        lax.fori_loop(0, 64, regroup, 0, unroll=8)
        write(c).start()

    pltpu.make_async_copy(relay, relay, onward_sem).wait()
    for ws, (z, p) in enumerate(((z12, p12), (z0, p0))):
        some = p.at[pl.ds(0, wide - 1)]
        pltpu.make_async_copy(some, some, p_send.at[ws]).wait()
        for c in range(len(CHUNKS)):
            some = piece(z, pl.ds(0, wide - 1), c)
            pltpu.make_async_copy(some, some, z_send.at[ws, c]).wait()
    for c in range(len(CHUNKS)):
        write(c).wait()


def lag_kernel(cross_hbm, lag_hbm, out_hbm, cross, lag, out, lag_sem, read_sem, write_sem):
    channels, parts = cross.shape[0], 4
    each = channels // parts

    def read(q):
        at = pl.ds(q * each, each)
        return pltpu.make_async_copy(cross_hbm.at[at], cross.at[at], read_sem.at[q])

    def write(q):
        at = pl.ds(q * each, each)
        return pltpu.make_async_copy(out.at[:, at], out_hbm.at[:, at], write_sem.at[q])

    table = pltpu.make_async_copy(lag_hbm, lag, lag_sem)
    table.start()
    for q in range(parts):
        read(q).start()
    table.wait()
    for q in range(parts):
        read(q).wait()
        for i in range(q * each, (q + 1) * each):
            x = cross[i].reshape(2 * BINS, 128)
            out[:, i] = dot(x, lag[...], TN).astype(BF).reshape(SLOTS, 32, LAGS)
        write(q).start()
    for q in range(parts):
        write(q).wait()


def on_device(records, taps, pair_sources, pair_counts):
    blocks, channels, _ = records.shape
    any_spec = pl.BlockSpec(memory_space=pl.ANY)
    smem = pl.BlockSpec(memory_space=pltpu.SMEM)
    forward = forward_table()
    extract = np.zeros((16, 256), ml_dtypes.bfloat16)
    extract[np.arange(16), np.arange(16) * 16] = 1
    repeat = np.zeros((512, 32), ml_dtypes.bfloat16)
    repeat[np.arange(512), np.arange(512) // 16] = 1
    perm = np.zeros((128, 128), ml_dtypes.bfloat16)
    for col in range(128):
        k, v = col // 32, col % 32
        perm[(v // 4) * 16 + k * 4 + v % 4, col] = 1
    shift = np.zeros((PAST, HALF), ml_dtypes.bfloat16)
    shift[np.arange(PAST), HALF - PAST + np.arange(PAST)] = 1
    dma = pltpu.SemaphoreType.DMA
    vm = lambda *shape, dtype=BF: pltpu.VMEM(shape, dtype)
    cross = pl.pallas_call(
        whole_kernel,
        out_shape=jax.ShapeDtypeStruct((channels, 2, BINS, 128), BF),
        in_specs=[smem] + [any_spec] * 9,
        out_specs=any_spec,
        scratch_shapes=[
            vm(1, TAPS, dtype=F32), vm(SLOTS, 32, dtype=jnp.int32), vm(512, 256), vm(256, 512), vm(16, 256),
            vm(512, 32), vm(128, 128), vm(PAST, HALF), vm(1, 1024, dtype=F32), vm(512, 256), vm(512, 128),
            vm(8, 128, dtype=F32),
            vm(blocks, channels, 1536), vm(PAST, blocks * channels), vm(PAST, blocks * channels), vm(128, HALF),
            vm(32, 2, 128, 128), vm(32, 128, 128), vm(32, 2, 128, 128), vm(32, 128, 128), vm(128, 1536),
            vm(32, 16, 512), vm(32, 16, 256), vm(8, 32, 16, 512), vm(8, 32, 16, 256),
            vm(97 * PITCH, 128, dtype=F32), vm(2, 97 * PITCH, 128, dtype=F32), vm((BINS + 1) * PITCH, 128, dtype=F32),
            vm(channels, 2, BINS, 128), vm(4, 2, CHUNKS[0][1], 128),
            dma((8,)), dma((9,)), dma((2,)), dma((2, len(CHUNKS))), dma((2, len(CHUNKS))), dma((2,)), dma((2,)), dma((4,)),
            dma((2, 4)), dma((2, 4)), dma((2, 4)), dma((2, 4)), dma, dma, dma((len(CHUNKS),))],
        compiler_params=pltpu.CompilerParams(collective_id=0, has_side_effects=True, vmem_limit_bytes=62 << 20),
        name="cross",
    )(pair_counts, records, taps.reshape(1, TAPS), pair_sources.T, jnp.asarray(forward), jnp.asarray(forward.T),
      jnp.asarray(extract), jnp.asarray(repeat), jnp.asarray(perm), jnp.asarray(shift))
    out = pl.pallas_call(
        lag_kernel,
        out_shape=jax.ShapeDtypeStruct((SLOTS, channels, 32, LAGS), BF),
        in_specs=[any_spec, any_spec],
        out_specs=any_spec,
        scratch_shapes=[
            vm(channels, 2, BINS, 128), vm(2 * BINS, LAGS), vm(SLOTS, channels, 32, LAGS), dma, dma((4,)), dma((4,))],
        compiler_params=pltpu.CompilerParams(vmem_limit_bytes=60 << 20),
        name="lags",
    )(cross, jnp.asarray(lag_table()))
    return out[None]


def solution(mesh):
    return jax.shard_map(
        on_device,
        mesh=mesh,
        in_specs=(P(None, "narrow", "wide"), P(), P(), P("wide")),
        out_specs=P("wide", None, "narrow", None, None),
        check_vma=False,
    )
```
